32 devices in a mesh: col: 8 (over z, x), rhs: 4 (over y, core).
Axes of the slice: x: 2, y: 2, z: 4, core: 2. Of those that a mesh axis runs over, the one named last changes fastest.
Arguments:
- rhs_block: bfloat16 [2048, 4096], P('col', 'rhs'), may hold values from -6 to 6
- solution: bfloat16 [24576, 4096], P('col', 'rhs'), may hold values from -6 to 6
- factor: bfloat16 [8, 6, 256, 3072], P('col', None, 'rhs'), may hold values from -0.109375 to 0.109375
- tile_list: int32 [8, 6], P('col'), may hold values 0 or 1
- diag_inverse: bfloat16 [8, 256, 256], P('col'), may hold values from -0.375 to 0.375
Outputs:
- solved_rows: bfloat16 [2048, 4096], P('col', 'rhs')
The draws below stay inside these ranges and needn't reach their ends.
All inputs are finite; a program needn't handle non-finite values. No bound on the sum of `tile_list` on one device may be relied on, other than what follows from the above.
Results may differ from the reference program's by a relative error of at most 0.0049.
Values may be sent and summed in bfloat16 or wider, within the bound.
No kernel may reach another device: no remote copies, remote signals or barrier semaphores. Data moves between devices by JAX's collectives and lax.ppermute only.
A program may use at most 64 MiB of HBM per device.

```python
import jax
import jax.numpy as jnp
from jax import lax

BS = 256
XB = 1536
OWN_BLOCKS = 2
NRHS = 4096
HOPS = 6
ROWS = 2048
SOL_ROWS = 24576
N_COL = 8


def touch_ends(values, stream_key, least, high):
    longest = values.shape.index(max(values.shape))
    spots = []
    for shift in (0, 1):
        where = [jax.random.randint(jax.random.fold_in(stream_key, axis), (), 0, length) for axis, length in enumerate(values.shape)]
        where[longest] = (where[longest] + shift) % values.shape[longest]
        spots.append(tuple(where))
    return values.at[spots[0]].set(least).at[spots[1]].set(high)


def block_levels(stream_key, shape, cuts, least, high):
    factor_of = 1.0
    for position, blocks in cuts:
        heights = jax.random.uniform(jax.random.fold_in(jax.random.fold_in(stream_key, 6), position), (blocks,), jnp.float32, least / len(cuts), high / len(cuts))
        factor_of = factor_of * jnp.repeat(jnp.exp(heights), shape[position] // blocks).reshape((-1,) + (1,) * (len(shape) - 1 - position))
    return factor_of


def gaussian(key, shape, spread, reach, cuts=(), kind=jnp.bfloat16):
    factor_of = block_levels(key, shape, cuts, -0.22, 0.18) if cuts else 1.0
    result = jax.random.normal(key, shape, jnp.float32) * spread * factor_of
    return jnp.minimum(jnp.maximum(result, -reach), reach).astype(kind)


def setup_inputs(seed: int = 0) -> dict:
    key_list = jax.random.split(jax.random.key(seed), 6)
    rhs_block = gaussian(key_list[0], (ROWS, NRHS), 1.0, 6.0, ((0, 8), (1, 4)))
    solution = gaussian(key_list[1], (SOL_ROWS, NRHS), 1.0, 6.0, ((0, 8), (1, 4)))
    factor = gaussian(key_list[2], (N_COL, HOPS, BS, OWN_BLOCKS * XB), (OWN_BLOCKS * XB) ** -0.5, 0.109375, ((0, 8), (2, 4)))
    tile_list = touch_ends((jax.random.randint(key_list[3], (N_COL, HOPS), 0, 4) < 3).astype(jnp.int32), jax.random.fold_in(key_list[3], 1), 0, 1)
    diag_inverse = gaussian(key_list[4], (N_COL, BS, BS), BS ** -0.5, 0.375, ((0, 8),))
    return {"rhs_block": rhs_block, "solution": solution, "factor": factor, "tile_list": tile_list, "diag_inverse": diag_inverse}


def reference(rhs_block, solution, factor, tile_list, diag_inverse):
    owners = jnp.arange(N_COL, dtype=jnp.int32)
    weights = tile_list.astype(jnp.float32)
    solved = solution.reshape(N_COL, OWN_BLOCKS * XB, NRHS)
    rhs_rows = rhs_block.reshape(N_COL, BS, NRHS)

    def one_row(exit_row):
        total = jnp.zeros((BS, NRHS), jnp.float32)
        for offset in range(HOPS):
            source = ((exit_row - offset - 1 + N_COL) % N_COL).astype(jnp.int32)
            product = jnp.dot(factor[source, offset], solved[source], preferred_element_type=jnp.float32)
            total = total + product * weights[source, offset]
        remaining = (rhs_rows[exit_row].astype(jnp.float32) - total).astype(jnp.bfloat16)
        return jnp.dot(diag_inverse[exit_row], remaining, preferred_element_type=jnp.float32).astype(jnp.bfloat16)

    blocks = lax.map(one_row, owners)
    return blocks.reshape(N_COL * BS, NRHS)
```

```python
import jax
import jax.numpy as jnp
from jax import lax
from jax.sharding import PartitionSpec as P


def shift(block, axis, distance):
    size = lax.axis_size(axis)
    return lax.ppermute(block, axis, [(i, (i + distance) % size) for i in range(size)])


def pair_swap(block, axis):
    size = lax.axis_size(axis)
    return lax.ppermute(block, axis, [(i, i ^ 1) for i in range(size)])


def across(block, axis):
    return shift(block, axis, lax.axis_size(axis) // 2)


def half_gather(block, axis):
    size = lax.axis_size(axis)
    half = size // 2
    parts = [block]
    for j in range(1, half):
        route = [(i // half * half + (i % half + j) % half, i) for i in range(size)]
        parts.append(lax.ppermute(block, axis, route))
    return parts


def per_device(rhs_block, solution, factor, tile_list, diag_inverse):
    hops, quarter, depth = factor.shape[1:]
    rows, cols = rhs_block.shape
    stages = hops // 2
    odd = lax.axis_index("col") % 2 == 1
    size = lax.axis_size("rhs")
    half = size // 2
    me = lax.axis_index("rhs")
    tiles = factor[0]
    weight = tile_list[0].astype(jnp.float32)

    def give(array, d):
        return jnp.where(odd, array[2 * (d - 1)], array[2 * (d % stages)])

    def own(array, d):
        return array[2 * d - 1]

    def product(left, scale):
        out = jnp.dot(left, solution, preferred_element_type=jnp.float32)
        return out * scale

    order = [2, 3, 1] if stages == 3 else list(range(stages, 0, -1))
    far = {}
    for d in order:
        far[d] = (across(give(tiles, d), "rhs"), across(own(tiles, d), "rhs"))

    near = [product(part, jnp.repeat(weight, quarter)[:, None]).reshape(hops, quarter, cols)
            for part in half_gather(tiles.reshape(hops * quarter, depth), "rhs")]
    near_give = {d: jnp.concatenate([give(p, d) for p in near]).astype(jnp.bfloat16) for d in order}
    near_own = {d: jnp.concatenate([own(p, d) for p in near]) for d in order}

    def far_products(d):
        g = jnp.concatenate(half_gather(far[d][0], "rhs"))
        o = jnp.concatenate(half_gather(far[d][1], "rhs"))
        return product(g, give(weight, d)).astype(jnp.bfloat16), product(o, own(weight, d))

    def combine(d, mine, received, extra=None):
        received = received.astype(jnp.float32)
        stay = None
        if d == stages:
            stay = jnp.where(odd, received, 0.0)
            received = jnp.where(odd, 0.0, received)
        total = mine + received
        if extra is not None:
            total = total + extra.astype(jnp.float32)
        return total.astype(jnp.bfloat16), stay

    def reduce(gives, owns):
        arrived = jnp.zeros((half * quarter, cols), jnp.float32)
        chained = None
        for d in order:
            received = pair_swap(gives[d], "col")
            total, stay = combine(d, owns[d], received, chained if d == 1 else None)
            if d == 2:
                chained = shift(total, "col", 2)
            else:
                arrived = arrived + shift(total, "col", 2 * d).astype(jnp.float32)
            if stay is not None:
                arrived = arrived + stay
        return arrived

    near_sum = reduce(near_give, near_own)
    far_give, far_own = {}, {}
    for d in order:
        far_give[d], far_own[d] = far_products(d)
    far_sum = reduce(far_give, far_own)

    place = jnp.concatenate([
        (((me // half + s) % 2) * half + (me % half + j) % half) * quarter + jnp.arange(quarter)
        for s in range(2) for j in range(half)
    ])
    pick = (lax.broadcasted_iota(jnp.int32, (rows, rows), 0) == place[None, :]).astype(jnp.bfloat16)
    rhs_local = jnp.dot(pick.T, rhs_block, preferred_element_type=jnp.float32)
    diag_local = jnp.dot(diag_inverse[0], pick, preferred_element_type=jnp.float32).astype(jnp.bfloat16)
    acc = jnp.concatenate([near_sum, far_sum])
    remaining = (rhs_local - acc).astype(jnp.bfloat16)
    return jnp.dot(diag_local, remaining, preferred_element_type=jnp.float32).astype(jnp.bfloat16)


def solution(mesh):
    in_specs = (
        P("col", "rhs"),
        P("col", "rhs"),
        P("col", None, "rhs", None),
        P("col", None),
        P("col", None, None),
    )
    out_specs = P("col", "rhs")
    return jax.shard_map(
        per_device, mesh=mesh, in_specs=in_specs, out_specs=out_specs, check_vma=False
    )
```

```python
import functools

import jax
import jax.numpy as jnp
from jax import lax
from jax.experimental import pallas as pl
from jax.experimental.pallas import tpu as pltpu
from jax.sharding import PartitionSpec as P

F32, BF16 = jnp.float32, jnp.bfloat16
VMEM = pl.BlockSpec(memory_space=pltpu.VMEM)
SMEM = pl.BlockSpec(memory_space=pltpu.SMEM)
ANY = pl.BlockSpec(memory_space=pl.ANY)
HBM = pl.BlockSpec(memory_space=pltpu.HBM)


WIDE = 256
PIECES = 4


def shift(block, axis, distance):
    size = lax.axis_size(axis)
    return lax.ppermute(block, axis, [(i, (i + distance) % size) for i in range(size)])


def pair_swap(block, axis):
    size = lax.axis_size(axis)
    return lax.ppermute(block, axis, [(i, i ^ 1) for i in range(size)])


def across(block, axis):
    return shift(block, axis, lax.axis_size(axis) // 2)


def inner(i, j, half):
    return i // half * half + (i % half + j) % half


def half_gather(block, axis):
    size = lax.axis_size(axis)
    half = size // 2
    parts = [block]
    for j in range(1, half):
        parts.append(lax.ppermute(block, axis, [(inner(i, j, half), i) for i in range(size)]))
    return parts


def to_columns(blocks, distance):
    n, size = lax.axis_size("col"), lax.axis_size("rhs")
    out = []
    for j, block in enumerate(blocks):
        route = [(c * size + r, (c + distance) % n * size + inner(r, j, size // 2))
                 for c in range(n) for r in range(size)]
        out.append(lax.ppermute(block, ("col", "rhs"), route) if distance or j else block)
    return out


def pinned(*shape, dtype=BF16):
    return pltpu.VMEM(shape, dtype)


def call(body, outs, specs, args, flops=0, space=12, out_specs=None, **more):
    moved = sum(a.size * a.dtype.itemsize for a in args)
    return pl.pallas_call(
        body,
        out_shape=outs,
        in_specs=specs,
        out_specs=out_specs or [VMEM] * len(outs),
        compiler_params=pltpu.CompilerParams(vmem_limit_bytes=space << 20),
        cost_estimate=pl.CostEstimate(flops=flops, bytes_accessed=moved, transcendentals=0),
        **more,
    )(*args)


def take(tiles, groups, *earlier):
    n, rows = len(groups), tiles.shape[1]

    def body(*refs):
        src, dsts, sems = refs[0], refs[-1 - n:-1], refs[-1]
        copies = []
        for group, dst in zip(groups, dsts):
            for i, k in enumerate(group):
                for at in range(0, rows, rows // PIECES):
                    cut = pl.ds(at, rows // PIECES)
                    copies.append(pltpu.make_async_copy(src.at[k, cut], dst.at[i, cut], sems.at[len(copies)]))
        for c in copies:
            c.start()
        for c in copies:
            c.wait()

    outs = [pinned(len(g), *tiles.shape[1:]) for g in groups]
    return call(body, outs, [HBM] + [ANY] * len(earlier), [in_hbm(tiles), *earlier], space=2,
                scratch_shapes=[pltpu.SemaphoreType.DMA((PIECES * sum(map(len, groups)),))])


def in_hbm(array):
    return pltpu.with_memory_space_constraint(array, pltpu.HBM)


def on_odd():
    return lax.rem(lax.axis_index("col"), 2) == 1


def gate(block, *earlier):
    def body(*refs):
        pass

    return call(body, [jax.ShapeDtypeStruct(block.shape, block.dtype)], [ANY] * (1 + len(earlier)), [block, *earlier],
                space=1, out_specs=[ANY], input_output_aliases={0: 0})[0]


def column_cuts(cols):
    wide = min(WIDE, cols)
    return [slice(at, at + wide) for at in range(0, cols, wide)]


def per_device(rhs_block, solution, factor, tile_list, diag_inverse):
    hops, quarter, depth = factor.shape[1:]
    rows, cols = rhs_block.shape
    size = lax.axis_size("rhs")
    half = size // 2
    tiles = factor[0]
    gives, owns = (2, 4, 0), (3, 5, 1)
    cuts = column_cuts(cols)
    strip = (half, quarter, cols)
    one = pinned(*strip)

    s24, = take(tiles, [(2, 4)])
    y24 = across(s24, "rhs")
    others = half_gather(solution, "rhs")[1:]
    s35, s0, s1 = take(tiles, [(3, 5), (0,), (1,)], s24)
    y35 = across(s35, "rhs")
    y0 = across(s0, "rhs")
    y1 = across(s1, "rhs")

    def near(left_ref, sol, weights, *refs):
        give, own = refs[-2:]
        left = left_ref[...].reshape(hops * quarter, depth)
        for cut in cuts:
            total = jnp.dot(left, sol[:, cut], preferred_element_type=F32)
            for i in range(len(gives)):
                g = total[gives[i] * quarter:(gives[i] + 1) * quarter]
                give[i, :, cut] = (g * weights[0, gives[i]].astype(F32)).astype(BF16)
                o = total[owns[i] * quarter:(owns[i] + 1) * quarter]
                own[i, :, cut] = o * weights[0, owns[i]].astype(F32)

    sols = [solution, *others]
    near_own, got_near = [], []
    token = s35
    for sol in sols:
        give, own = call(near, [pinned(3, quarter, cols), pinned(3, quarter, cols, dtype=F32)],
                         [VMEM, VMEM, SMEM, ANY], [tiles, sol, tile_list, token],
                         flops=2 * hops * quarter * depth * cols)
        got_near.append(pair_swap(give, "col"))
        near_own.append(own)
        token = own

    def products(far, ks, epilogue, outs, extra, earlier, which=None):
        which = list(range(half)) if which is None else which
        n_sol, n_extra = len(which), len(extra)

        def body(far_ref, *refs):
            sol_refs, weights = refs[:n_sol], refs[n_sol]
            more = refs[n_sol + 1:n_sol + 1 + n_extra]
            out = refs[len(refs) - len(outs):]
            is_odd = on_odd()
            left = far_ref[...].reshape(len(ks) * quarter, depth)
            for part, sol_ref in zip(which, sol_refs):
                for cut in cuts:
                    total = jnp.dot(left, sol_ref[:, cut], preferred_element_type=F32)
                    for i, k in enumerate(ks):
                        term = total[i * quarter:(i + 1) * quarter] * weights[0, k].astype(F32)
                        epilogue(out, more, is_odd, i, part, cut, term)

        args = [far, *[sols[p] for p in which], tile_list, *extra, *earlier]
        specs = [VMEM] * (n_sol + 1) + [SMEM] + [VMEM] * n_extra + [ANY] * len(earlier)
        return call(body, outs, specs, args, flops=2 * len(ks) * quarter * depth * cols * n_sol)

    def store(out, more, is_odd, i, part, cut, total):
        out[0][i, part, :, cut] = total.astype(out[0].dtype)

    far_give, = products(y24, (2, 4), store, [pinned(2, *strip)], [], [token])
    got_far = pair_swap(far_give, "col")

    def near23(*refs):
        owns, gots, (d2, d3) = refs[:half], refs[half:2 * half], refs[-2:]
        is_odd = on_odd()
        for part, (own, got) in enumerate(zip(owns, gots)):
            r4 = got[1].astype(F32)
            d2[part] = (own[0] + jnp.where(is_odd, r4, got[0].astype(F32))).astype(BF16)
            d3[part] = (own[1] + jnp.where(is_odd, 0.0, r4)).astype(BF16)

    d2n, d3n = call(near23, [one, one], [VMEM] * (2 * half) + [ANY], [*near_own, *got_near, far_give])
    d2n_in = shift(d2n, "col", 2)
    d3n_in = shift(d3n, "col", 6)

    def near1(chained, *refs):
        owns, gots, d1 = refs[:half], refs[half:2 * half], refs[-1]
        is_odd = on_odd()
        for part, (own, got) in enumerate(zip(owns, gots)):
            r = jnp.where(is_odd, got[0].astype(F32), got[2].astype(F32))
            d1[part] = (own[2] + r + chained[part].astype(F32)).astype(BF16)

    d1n, = call(near1, [one], [VMEM] * (1 + 2 * half), [d2n_in, *near_own, *got_near])
    d1n_in = shift(d1n, "col", 2)

    def far23(out, more, is_odd, i, part, cut, total):
        got, = more
        r4 = got[1, part, :, cut].astype(F32)
        if i == 0:
            total = total + jnp.where(is_odd, r4, got[0, part, :, cut].astype(F32))
        else:
            total = total + jnp.where(is_odd, 0.0, r4)
        out[i][part, :, cut] = total.astype(BF16)

    d2f, d3f = products(y35, (3, 5), far23, [one, one], [got_far], [d1n])
    d2f_in = shift(d2f, "col", 2)
    d3f_in = shift(d3f, "col", 6)

    last_give, = products(y0, (0,), store, [pinned(1, *strip)], [], [d2f])
    got_last = pair_swap(last_give, "col")

    def collect(d1, d3, gl, d3far, *refs):
        gots, outs = refs[:half], refs[-half:]
        is_odd = on_odd()
        for part, (got, out) in enumerate(zip(gots, outs)):
            upper = d1[part].astype(F32) + d3[part].astype(F32)
            out[0] = upper + jnp.where(is_odd, got[2].astype(F32), 0.0)
            out[1] = d3far[part].astype(F32) + jnp.where(is_odd, gl[0, part].astype(F32), 0.0)

    sums = call(collect, [pinned(2, quarter, cols, dtype=F32)] * half, [VMEM] * (4 + half) + [ANY],
                [d1n_in, d3n_in, got_last, d3f_in, *got_near, last_give])
    sums_in = to_columns(sums, 0)

    def far1(out, more, is_odd, i, part, cut, total):
        got, got0, chained = more
        r = jnp.where(is_odd, got[0, part, :, cut].astype(F32), got0[0, part, :, cut].astype(F32))
        out[0][:, cut] = (total + r + chained[part, :, cut].astype(F32)).astype(BF16)

    d1f = [None] * half
    token = sums[-1]
    for part in list(range(1, half)) + [0]:
        d1f[part], = products(y1, (1,), far1, [pinned(quarter, cols)], [got_far, got_last, d2f_in], [token], [part])
        token = d1f[part]
    d1f_in = to_columns(d1f, 2)

    def arrange(rhs, diag, _, rhs_out, diag_out):
        me = lax.axis_index("rhs")
        upper, mine = lax.div(me, half), lax.rem(me, half)
        column = lax.broadcasted_iota(jnp.int32, (rows, rows), 1)
        source = column
        for s in range(2):
            for j in range(half):
                at = (s * half + j) * quarter
                block = lax.rem(upper + s, 2) * half + lax.rem(mine + half - j, half)
                start = pl.multiple_of(block * quarter, quarter)
                rhs_out[at:at + quarter] = rhs[pl.ds(start, quarter)]
                source = jnp.where((column >= at) & (column < at + quarter), column - at + start, source)
        pick = (lax.broadcasted_iota(jnp.int32, (rows, rows), 0) == source).astype(BF16)
        diag_out[...] = jnp.dot(diag[0], pick, preferred_element_type=F32).astype(BF16)

    rhs_local, diag_local = call(arrange, [pinned(rows, cols), pinned(rows, rows)], [VMEM, VMEM, ANY],
                                 [rhs_block, diag_inverse, near_own[-1]], flops=2 * rows * rows * rows)

    def final(rhs, diag, *refs):
        acc, last, out = refs[:half], refs[half:2 * half], refs[-1]
        total = jnp.concatenate([a[0] for a in acc] + [a[1] + l[...].astype(F32) for a, l in zip(acc, last)])
        remaining = (rhs[...].astype(F32) - total).astype(BF16)
        out[...] = jnp.dot(diag[...], remaining, preferred_element_type=F32).astype(BF16)

    return call(final, [jax.ShapeDtypeStruct((rows, cols), BF16)], [VMEM] * (2 + 2 * half),
                [rhs_local, diag_local, *sums_in, *d1f_in], flops=2 * rows * rows * cols)[0]


def solution(mesh):
    in_specs = (
        P("col", "rhs"),
        P("col", "rhs"),
        P("col", None, "rhs", None),
        P("col", None),
        P("col", None, None),
    )
    out_specs = P("col", "rhs")
    return jax.shard_map(
        per_device, mesh=mesh, in_specs=in_specs, out_specs=out_specs, check_vma=False
    )
```

```python
import functools

import jax
import jax.numpy as jnp
from jax import lax
from jax.experimental import pallas as pl
from jax.experimental.pallas import tpu as pltpu
from jax.sharding import PartitionSpec as P

F32, BF16 = jnp.float32, jnp.bfloat16
VMEM = pl.BlockSpec(memory_space=pltpu.VMEM)
SMEM = pl.BlockSpec(memory_space=pltpu.SMEM)
ANY = pl.BlockSpec(memory_space=pl.ANY)
HBM = pl.BlockSpec(memory_space=pltpu.HBM)


WIDE = 256
PIECES = 4


def shift(block, axis, distance):
    size = lax.axis_size(axis)
    return lax.ppermute(block, axis, [(i, (i + distance) % size) for i in range(size)])


def pair_swap(block, axis):
    size = lax.axis_size(axis)
    return lax.ppermute(block, axis, [(i, i ^ 1) for i in range(size)])


def across(block, axis):
    return shift(block, axis, lax.axis_size(axis) // 2)


def inner(i, j, half):
    return i // half * half + (i % half + j) % half


def half_gather(block, axis):
    size = lax.axis_size(axis)
    half = size // 2
    parts = [block]
    for j in range(1, half):
        parts.append(lax.ppermute(block, axis, [(inner(i, j, half), i) for i in range(size)]))
    return parts


def to_columns(blocks, distance):
    n, size = lax.axis_size("col"), lax.axis_size("rhs")
    out = []
    for j, block in enumerate(blocks):
        route = [(c * size + r, (c + distance) % n * size + inner(r, j, size // 2))
                 for c in range(n) for r in range(size)]
        out.append(lax.ppermute(block, ("col", "rhs"), route) if distance or j else block)
    return out


def pinned(*shape, dtype=BF16):
    return pltpu.VMEM(shape, dtype)


def call(body, outs, specs, args, flops=0, space=12, out_specs=None, **more):
    moved = sum(a.size * a.dtype.itemsize for a in args)
    return pl.pallas_call(
        body,
        out_shape=outs,
        in_specs=specs,
        out_specs=out_specs or [VMEM] * len(outs),
        compiler_params=pltpu.CompilerParams(vmem_limit_bytes=space << 20),
        cost_estimate=pl.CostEstimate(flops=flops, bytes_accessed=moved, transcendentals=0),
        **more,
    )(*args)


def take(tiles, groups, *earlier):
    n, rows = len(groups), tiles.shape[1]

    def body(*refs):
        src, dsts, sems = refs[0], refs[-1 - n:-1], refs[-1]
        copies = []
        for group, dst in zip(groups, dsts):
            for i, k in enumerate(group):
                for at in range(0, rows, rows // PIECES):
                    cut = pl.ds(at, rows // PIECES)
                    copies.append(pltpu.make_async_copy(src.at[k, cut], dst.at[i, cut], sems.at[len(copies)]))
        for c in copies:
            c.start()
        for c in copies:
            c.wait()

    outs = [pinned(len(g), *tiles.shape[1:]) for g in groups]
    return call(body, outs, [HBM] + [ANY] * len(earlier), [in_hbm(tiles), *earlier], space=2,
                scratch_shapes=[pltpu.SemaphoreType.DMA((PIECES * sum(map(len, groups)),))])


def in_hbm(array):
    return pltpu.with_memory_space_constraint(array, pltpu.HBM)


def on_odd():
    return lax.rem(lax.axis_index("col"), 2) == 1


def gate(block, *earlier):
    def body(*refs):
        pass

    return call(body, [jax.ShapeDtypeStruct(block.shape, block.dtype)], [ANY] * (1 + len(earlier)), [block, *earlier],
                space=1, out_specs=[ANY], input_output_aliases={0: 0})[0]


def column_cuts(cols):
    wide = min(WIDE, cols)
    return [slice(at, at + wide) for at in range(0, cols, wide)]


def per_device(rhs_block, solution, factor, tile_list, diag_inverse):
    hops, quarter, depth = factor.shape[1:]
    rows, cols = rhs_block.shape
    size = lax.axis_size("rhs")
    half = size // 2
    tiles = factor[0]
    gives, owns = (2, 4, 0), (3, 5, 1)
    cuts = column_cuts(cols)
    strip = (half, quarter, cols)
    one = pinned(*strip)

    s24, = take(tiles, [(2, 4)])
    y24 = across(s24, "rhs")
    others = half_gather(solution, "rhs")[1:]
    s35, s0, s1 = take(tiles, [(3, 5), (0,), (1,)], s24)
    y35 = across(s35, "rhs")
    y0 = across(s0, "rhs")
    y1 = across(s1, "rhs")
    taken, order = [s24, s35, s0, s1], (2, 4, 3, 5, 0, 1)

    def near(*refs):
        lefts, (sol, weights), (give, own) = refs[:len(taken)], refs[len(taken):len(taken) + 2], refs[-2:]
        left = jnp.concatenate([r[i] for r in lefts for i in range(r.shape[0])])
        for cut in cuts:
            total = jnp.dot(left, sol[:, cut], preferred_element_type=F32)
            for at, k in enumerate(order):
                term = total[at * quarter:(at + 1) * quarter] * weights[0, k].astype(F32)
                if k in gives:
                    give[gives.index(k), :, cut] = term.astype(BF16)
                else:
                    own[owns.index(k), :, cut] = term

    sols = [solution, *others]
    near_own, got_near = [], []
    token = s35
    for sol in sols:
        give, own = call(near, [pinned(3, quarter, cols), pinned(3, quarter, cols, dtype=F32)],
                         [VMEM] * (len(taken) + 1) + [SMEM, ANY], [*taken, sol, tile_list, token],
                         flops=2 * hops * quarter * depth * cols)
        got_near.append(pair_swap(give, "col"))
        near_own.append(own)
        token = own

    def products(far, ks, epilogue, outs, extra, earlier, which=None):
        which = list(range(half)) if which is None else which
        n_sol, n_extra = len(which), len(extra)

        def body(far_ref, *refs):
            sol_refs, weights = refs[:n_sol], refs[n_sol]
            more = refs[n_sol + 1:n_sol + 1 + n_extra]
            out = refs[len(refs) - len(outs):]
            is_odd = on_odd()
            left = far_ref[...].reshape(len(ks) * quarter, depth)
            for part, sol_ref in zip(which, sol_refs):
                for cut in cuts:
                    total = jnp.dot(left, sol_ref[:, cut], preferred_element_type=F32)
                    for i, k in enumerate(ks):
                        term = total[i * quarter:(i + 1) * quarter] * weights[0, k].astype(F32)
                        epilogue(out, more, is_odd, i, part, cut, term)

        args = [far, *[sols[p] for p in which], tile_list, *extra, *earlier]
        specs = [VMEM] * (n_sol + 1) + [SMEM] + [VMEM] * n_extra + [ANY] * len(earlier)
        return call(body, outs, specs, args, flops=2 * len(ks) * quarter * depth * cols * n_sol)

    def store(out, more, is_odd, i, part, cut, total):
        out[0][i, part, :, cut] = total.astype(out[0].dtype)

    far_give, = products(y24, (2, 4), store, [pinned(2, *strip)], [], [token])
    got_far = pair_swap(far_give, "col")

    def near23(*refs):
        owns, gots, (d2, d3) = refs[:half], refs[half:2 * half], refs[-2:]
        is_odd = on_odd()
        for part, (own, got) in enumerate(zip(owns, gots)):
            r4 = got[1].astype(F32)
            d2[part] = (own[0] + jnp.where(is_odd, r4, got[0].astype(F32))).astype(BF16)
            d3[part] = (own[1] + jnp.where(is_odd, 0.0, r4)).astype(BF16)

    d2n, d3n = call(near23, [one, one], [VMEM] * (2 * half) + [ANY], [*near_own, *got_near, far_give])
    d2n_in = shift(d2n, "col", 2)
    d3n_in = shift(d3n, "col", 6)

    def near1(chained, *refs):
        owns, gots, d1 = refs[:half], refs[half:2 * half], refs[-1]
        is_odd = on_odd()
        for part, (own, got) in enumerate(zip(owns, gots)):
            r = jnp.where(is_odd, got[0].astype(F32), got[2].astype(F32))
            d1[part] = (own[2] + r + chained[part].astype(F32)).astype(BF16)

    d1n, = call(near1, [one], [VMEM] * (1 + 2 * half), [d2n_in, *near_own, *got_near])
    d1n_in = shift(d1n, "col", 2)

    def far23(out, more, is_odd, i, part, cut, total):
        got, = more
        r4 = got[1, part, :, cut].astype(F32)
        if i == 0:
            total = total + jnp.where(is_odd, r4, got[0, part, :, cut].astype(F32))
        else:
            total = total + jnp.where(is_odd, 0.0, r4)
        out[i][part, :, cut] = total.astype(BF16)

    d2f, d3f = products(y35, (3, 5), far23, [one, one], [got_far], [d1n])
    d2f_in = shift(d2f, "col", 2)
    d3f_in = shift(d3f, "col", 6)

    def near3(d3, *refs):
        gots, sums = refs[:half], refs[-1]
        is_odd = on_odd()
        for part, got in enumerate(gots):
            sums[part] = d3[part].astype(F32) + jnp.where(is_odd, got[2].astype(F32), 0.0)

    wide_one = pinned(*strip, dtype=F32)
    near_sum, = call(near3, [wide_one], [VMEM] * (1 + half) + [ANY], [d3n_in, *got_near, d2f])

    last_give, = products(y0, (0,), store, [pinned(1, *strip)], [], [near_sum])
    got_last = pair_swap(last_give, "col")

    def near_all(d1, sums, d2far, gf, _, total, pre):
        is_odd = on_odd()
        for part in range(half):
            total[part] = d1[part].astype(F32) + sums[part]
            pre[part] = d2far[part].astype(F32) + jnp.where(is_odd, gf[0, part].astype(F32), 0.0)

    near_total, pre = call(near_all, [wide_one, wide_one], [VMEM] * 4 + [ANY],
                           [d1n_in, near_sum, d2f_in, got_far, last_give])

    def plain(out, more, is_odd, i, part, cut, total):
        out[0][:, cut] = total

    raw, token = [], pre
    for part in range(1, half):
        term, = products(y1, (1,), plain, [pinned(quarter, cols, dtype=F32)], [], [token], [part])
        raw.append(term)
        token = term

    def collect(total, pre, gl, d3far, *refs):
        raws, refs = refs[:half - 1], refs[half:]
        pre0, sums, lasts = refs[0], refs[1:1 + half], refs[1 + half:]
        is_odd = on_odd()
        for part in range(half):
            r0 = gl[0, part].astype(F32)
            sums[part][0] = total[part]
            sums[part][1] = d3far[part].astype(F32) + jnp.where(is_odd, r0, 0.0)
            chained = pre[part] + jnp.where(is_odd, 0.0, r0)
            if part:
                lasts[part - 1][...] = (raws[part - 1][...] + chained).astype(BF16)
            else:
                pre0[...] = chained

    flat = pinned(quarter, cols, dtype=F32)
    pre0, *outs = call(
        collect, [flat] + [pinned(2, quarter, cols, dtype=F32)] * half + [pinned(quarter, cols)] * (half - 1),
        [VMEM] * (4 + half - 1) + [ANY], [near_total, pre, got_last, d3f_in, *raw, token])
    sums, lasts = outs[:half], outs[half:]
    sums_in = to_columns(sums, 0)

    def far1(out, more, is_odd, i, part, cut, total):
        out[0][:, cut] = (total + more[0][:, cut]).astype(BF16)

    own_last, = products(y1, (1,), far1, [pinned(quarter, cols)], [pre0], [], [0])
    last_in = to_columns([own_last, *lasts], 2)

    places = [(0, j) for j in range(half)] + [(1, j) for j in range(1, half)] + [(1, 0)]

    def arrange(rhs, diag, _, rhs_out, diag_out):
        me = lax.axis_index("rhs")
        upper, mine = lax.div(me, half), lax.rem(me, half)
        column = lax.broadcasted_iota(jnp.int32, (rows, rows), 1)
        source = column
        for slot, (s, j) in enumerate(places):
            at = slot * quarter
            block = lax.rem(upper + s, 2) * half + lax.rem(mine + half - j, half)
            start = pl.multiple_of(block * quarter, quarter)
            rhs_out[at:at + quarter] = rhs[pl.ds(start, quarter)]
            source = jnp.where((column >= at) & (column < at + quarter), column - at + start, source)
        pick = (lax.broadcasted_iota(jnp.int32, (rows, rows), 0) == source).astype(BF16)
        diag_out[...] = jnp.dot(diag[0], pick, preferred_element_type=F32).astype(BF16)

    rhs_local, diag_local = call(arrange, [pinned(rows, cols), pinned(rows, rows)], [VMEM, VMEM, ANY],
                                 [rhs_block, diag_inverse, near_own[-1]], flops=2 * rows * rows * rows)

    early = rows - quarter

    def most(rhs, diag, *refs):
        acc, last, out = refs[:half], refs[half:2 * half - 1], refs[-1]
        total = jnp.concatenate([a[0] for a in acc] + [a[1] + l[...].astype(F32) for a, l in zip(acc[1:], last)])
        remaining = (rhs[:early].astype(F32) - total).astype(BF16)
        out[...] = jnp.dot(diag[:, :early], remaining, preferred_element_type=F32)

    partial, = call(most, [pinned(rows, cols, dtype=F32)], [VMEM] * (2 + 2 * half - 1) + [ANY],
                    [rhs_local, diag_local, *sums_in, *last_in[1:], own_last], flops=2 * rows * early * cols)

    def final(rhs, diag, acc, last, part, out):
        total = acc[1] + last[...].astype(F32)
        remaining = (rhs[early:].astype(F32) - total).astype(BF16)
        out[...] = (part[...] + jnp.dot(diag[:, early:], remaining, preferred_element_type=F32)).astype(BF16)

    return call(final, [jax.ShapeDtypeStruct((rows, cols), BF16)], [VMEM] * 5,
                [rhs_local, diag_local, sums_in[0], last_in[0], partial], flops=2 * rows * quarter * cols)[0]


def solution(mesh):
    in_specs = (
        P("col", "rhs"),
        P("col", "rhs"),
        P("col", None, "rhs", None),
        P("col", None),
        P("col", None, None),
    )
    out_specs = P("col", "rhs")
    return jax.shard_map(
        per_device, mesh=mesh, in_specs=in_specs, out_specs=out_specs, check_vma=False
    )
```

```python
import functools

import jax
import jax.numpy as jnp
from jax import lax
from jax.experimental import pallas as pl
from jax.experimental.pallas import tpu as pltpu
from jax.sharding import PartitionSpec as P

F32, BF16 = jnp.float32, jnp.bfloat16
VMEM = pl.BlockSpec(memory_space=pltpu.VMEM)
SMEM = pl.BlockSpec(memory_space=pltpu.SMEM)
ANY = pl.BlockSpec(memory_space=pl.ANY)
HBM = pl.BlockSpec(memory_space=pltpu.HBM)


WIDE = 256
PIECES = 4
SPLIT = 2
FIRST2 = False
DIRECT_N, DIRECT_F = False, False
ORDER = (
    "rest", "p0a", "p0b", "p1a", "p1b", "n2", "f24", "n3", "n1", "gy1",
    "a3n", "f35", "gz1", "a1n", "f0", "f1a", "a2f", "f1", "a3f", "col",
)


def shift(block, axis, distance):
    size = lax.axis_size(axis)
    return lax.ppermute(block, axis, [(i, (i + distance) % size) for i in range(size)])


def pair_swap(block, axis):
    size = lax.axis_size(axis)
    return lax.ppermute(block, axis, [(i, i ^ 1) for i in range(size)])


def across(block, axis):
    return shift(block, axis, lax.axis_size(axis) // 2)


def inner(i, j, half):
    return i // half * half + (i % half + j) % half


def half_gather(block, axis):
    size = lax.axis_size(axis)
    half = size // 2
    parts = [block]
    for j in range(1, half):
        parts.append(lax.ppermute(block, axis, [(inner(i, j, half), i) for i in range(size)]))
    return parts


def to_columns(blocks, distance):
    n, size = lax.axis_size("col"), lax.axis_size("rhs")
    out = []
    for j, block in enumerate(blocks):
        route = [(c * size + r, (c + distance) % n * size + inner(r, j, size // 2))
                 for c in range(n) for r in range(size)]
        out.append(lax.ppermute(block, ("col", "rhs"), route) if distance or j else block)
    return out


def pinned(*shape, dtype=BF16):
    return pltpu.VMEM(shape, dtype)


def call(body, outs, specs, args, flops=0, space=12, out_specs=None, **more):
    moved = sum(a.size * a.dtype.itemsize for a in args)
    return pl.pallas_call(
        body,
        out_shape=outs,
        in_specs=specs,
        out_specs=out_specs or [VMEM] * len(outs),
        compiler_params=pltpu.CompilerParams(vmem_limit_bytes=space << 20),
        cost_estimate=pl.CostEstimate(flops=flops, bytes_accessed=moved, transcendentals=0),
        **more,
    )(*args)


def take(tiles, groups, *earlier, weights=None):
    n, rows, depth = len(groups), tiles.shape[1], tiles.shape[2]
    extra = [] if weights is None else [SMEM]

    def body(*refs):
        src, dsts, sems = refs[0], refs[-1 - n - len(extra):-1], refs[-1]
        copies = []
        for group, dst in zip(groups, dsts):
            for i, (k, begin, end) in enumerate(group):
                columns = pl.ds(begin, end - begin)
                for first in range(0, rows, rows // PIECES):
                    cut = pl.ds(first, rows // PIECES)
                    copies.append(pltpu.make_async_copy(src.at[k, cut, columns], dst.at[i, cut], sems.at[len(copies)]))
        for c in copies:
            c.start()
        if extra:
            for k in range(weights.shape[1]):
                dsts[-1][k:k + 1, :] = jnp.full((1, WIDE), refs[1][0, k].astype(F32))
        for c in copies:
            c.wait()

    outs = [pinned(len(g), rows, g[0][2] - g[0][1]) for g in groups]
    if extra:
        outs.append(pinned(weights.shape[1], WIDE, dtype=F32))
    return call(body, outs, [HBM] + extra + [ANY] * len(earlier),
                [in_hbm(tiles)] + ([] if weights is None else [weights]) + [*earlier], space=2,
                scratch_shapes=[pltpu.SemaphoreType.DMA((PIECES * sum(map(len, groups)),))])


def in_hbm(array):
    return pltpu.with_memory_space_constraint(array, pltpu.HBM)


def on_odd():
    return lax.rem(lax.axis_index("col"), 2) == 1


def gate(block, *earlier):
    def body(*refs):
        pass

    return call(body, [jax.ShapeDtypeStruct(block.shape, block.dtype)], [ANY] * (1 + len(earlier)), [block, *earlier],
                space=1, out_specs=[ANY], input_output_aliases={0: 0})[0]


def column_cuts(cols):
    wide = min(WIDE, cols)
    return [slice(at, at + wide) for at in range(0, cols, wide)]


def per_device(rhs_block, solution, factor, tile_list, diag_inverse):
    hops, quarter, depth = factor.shape[1:]
    rows, cols = rhs_block.shape
    size = lax.axis_size("rhs")
    half = size // 2
    tiles = factor[0]
    gives, owns = (2, 4, 0), (3, 5, 1)
    cuts = column_cuts(cols)
    strip = (half, quarter, cols)
    one, wide_one = pinned(*strip), pinned(*strip, dtype=F32)
    flat = pinned(quarter, cols)
    v = {}

    if FIRST2:
        s2, = take(tiles, [[(2, 0, depth)]])
        s4, = take(tiles, [[(4, 0, depth)]], s2)
        s24 = [s2, s4]
    else:
        s24 = list(take(tiles, [[(2, 0, depth), (4, 0, depth)]]))
    y24 = [across(s, "rhs") for s in s24]
    others = half_gather(solution, "rhs")[1:]
    cut_at = depth * SPLIT // 4
    last_tile = [[(1, 0, cut_at)], [(1, cut_at, depth)]] if SPLIT else [[(1, 0, depth)]]
    order = (3, 5, 0, 1)
    sols = [solution, *others]
    v["token"] = s24[-1]

    def chained(body, outs, ins, flops=0):
        n = len(ins)

        def run(*refs):
            body(*refs[:n], *refs[n + 1:])

        got = call(run, outs, [VMEM] * n + [ANY], [*ins, v["token"]], flops=flops)
        v["token"] = got[0]
        return got

    y, taken = {}, []

    def rest():
        s35, s0, *s1, v["weights"] = take(tiles, [[(3, 0, depth), (5, 0, depth)], [(0, 0, depth)]] + last_tile, v["token"],
                                          weights=tile_list)
        y[35] = across(s35, "rhs")
        y[0] = s0 if "gy0" in ORDER else across(s0, "rhs")
        y[1] = [s if g in ORDER else across(s, "rhs") for g, s in zip(("gy1", "gz1"), s1)]
        taken.extend([s35, s0, *s1])
        v["token"] = s35

    def gy0():
        y[0] = across(gate(y[0], v["token"]), "rhs")

    def gy1():
        y[1][0] = across(gate(y[1][0], v["token"]), "rhs")

    def gz1():
        y[1][1] = across(gate(y[1][1], v["token"]), "rhs")

    near_got, near_own, near_give0 = [], [], []

    def near_gives(part):
        def body(*refs):
            lefts, (sol, weights, _, give) = refs[:-4], refs[-4:]
            left = jnp.concatenate([r[i] for r in lefts for i in range(r.shape[0])])
            for cut in cuts:
                total = jnp.dot(left, sol[:, cut], preferred_element_type=F32)
                for i in range(2):
                    term = total[i * quarter:(i + 1) * quarter] * weights[gives[i]:gives[i] + 1, :total.shape[1]]
                    give[i, :, cut] = term.astype(BF16)

        got = call(body, [pinned(2, quarter, cols)], [VMEM] * (len(s24) + 2) + [ANY], [*s24, sols[part], v["weights"], v["token"]],
                   flops=4 * quarter * depth * cols)
        v["token"] = got[0]
        near_got.append(pair_swap(got[0], "col"))

    def near_rest(part):
        n = len(taken)
        joins = half - 1 if part == half - 1 else 0

        def body(*refs):
            lefts, (sol, weights), outs = refs[:n], refs[n:n + 2], refs[n + 3 + joins:]
            whole = [r[i] for r in lefts[:2] for i in range(r.shape[0])]
            left = jnp.concatenate(whole + [jnp.concatenate([r[0] for r in lefts[2:]], axis=1)])
            for cut in cuts:
                total = jnp.dot(left, sol[:, cut], preferred_element_type=F32)
                for at, k in enumerate(order):
                    term = total[at * quarter:(at + 1) * quarter] * weights[k:k + 1, :total.shape[1]]
                    if k in owns:
                        outs[0][owns.index(k), :, cut] = term
                    elif joins:
                        outs[1][part, :, cut] = term.astype(BF16)
                    else:
                        outs[1][:, cut] = term.astype(BF16)
            for p in range(joins):
                outs[1][p] = refs[n + 2 + p][...]

        got = call(body, [pinned(3, quarter, cols, dtype=F32), one if joins else flat],
                   [VMEM] * (n + 2 + joins) + [ANY],
                   [*taken, sols[part], v["weights"], *near_give0[:joins], v["token"]],
                   flops=8 * quarter * depth * cols)
        v["token"] = got[0]
        near_own.append(got[0])
        if joins:
            v["got0"] = pair_swap(got[1], "col")
        else:
            near_give0.append(got[1])

    def p0a():
        near_gives(0)

    def p0b():
        near_rest(0)

    def p1a():
        for part in range(1, half):
            near_gives(part)

    def p1b():
        for part in range(1, half):
            near_rest(part)

    def zeros():
        return [v["got0"]]

    def r0(refs, part):
        return refs[0][part].astype(F32)

    def products(far, ks, epilogue, outs, extra, deep=slice(None)):
        n_extra = len(extra)

        far = far if isinstance(far, list) else [far]
        n_far = len(far)

        def body(*refs):
            far_refs, refs = refs[:n_far], refs[n_far:]
            sol_refs, weights = refs[:half], refs[half]
            more = refs[half + 1:half + 1 + n_extra]
            out = refs[len(refs) - len(outs):]
            is_odd = on_odd()
            left = jnp.concatenate([r[i] for r in far_refs for i in range(r.shape[0])])
            for part, sol_ref in enumerate(sol_refs):
                for cut in cuts:
                    total = jnp.dot(left, sol_ref[deep, cut], preferred_element_type=F32)
                    for i, k in enumerate(ks):
                        term = total[i * quarter:(i + 1) * quarter] * weights[k:k + 1, :total.shape[1]]
                        epilogue(out, more, is_odd, i, part, cut, term)

        args = [*far, *sols, v["weights"], *extra, v["token"]]
        specs = [VMEM] * (n_far + half + 1 + n_extra) + [ANY]
        got = call(body, outs, specs, args, flops=2 * len(ks) * quarter * depth * cols * half)
        v["token"] = got[0]
        return got

    def store(out, more, is_odd, i, part, cut, total):
        out[0][i, part, :, cut] = total.astype(BF16)

    def plain(out, more, is_odd, i, part, cut, total):
        out[0][part, :, cut] = total

    def added(out, more, is_odd, i, part, cut, total):
        out[0][part, :, cut] = total + more[0][part, :, cut]

    def f24():
        def each(out, more, is_odd, i, part, cut, total):
            out[i][part, :, cut] = total.astype(BF16)

        v["got_far"] = [pair_swap(g, "col") for g in products(y24, (2, 4), each, [one, one], [])]

    def stage2(refs, d2):
        for p in range(half):
            own, got = refs[p], refs[half + p]
            d2[p] = (own[0] + jnp.where(on_odd(), got[1].astype(F32), got[0].astype(F32))).astype(BF16)

    def stage3(refs, d3):
        for p in range(half):
            own, got = refs[p], refs[half + p]
            d3[p] = (own[1] + jnp.where(on_odd(), 0.0, got[1].astype(F32))).astype(BF16)

    def stage1(refs, others, arrived, d1):
        for p in range(half):
            own, got = refs[p], refs[half + p]
            r = jnp.where(on_odd(), got[0].astype(F32), r0(others, p))
            total = own[2] + r
            d1[p] = (total if arrived is None else total + arrived[p].astype(F32)).astype(BF16)

    def send2(total, direct):
        return shift(total, "col", 4 if direct else 2)

    def n2():
        d2, = chained(lambda *refs: stage2(refs, refs[-1]), [one], [*near_own, *near_got])
        v["d2n"] = send2(d2, DIRECT_N)

    def n3():
        d3, = chained(lambda *refs: stage3(refs, refs[-1]), [one], [*near_own, *near_got])
        v["d3n"] = shift(d3, "col", 6)

    def n23():
        def body(*refs):
            stage2(refs, refs[-2])
            stage3(refs, refs[-1])

        d2, d3 = chained(body, [one, one], [*near_own, *near_got])
        v["d2n"], v["d3n"] = send2(d2, DIRECT_N), shift(d3, "col", 6)

    def n1():
        n = len(zeros())
        d1, = chained(lambda *refs: stage1(refs, refs[2 * half:2 * half + n], None if DIRECT_N else refs[-2], refs[-1]),
                      [one], [*near_own, *near_got, *zeros()] + ([] if DIRECT_N else [v["d2n"]]))
        v["d1n"] = shift(d1, "col", 2)

    def n1p():
        def body(*refs):
            for p in range(half):
                refs[-1][p] = refs[p][2] + refs[half][p].astype(F32)

        v["part1"], = chained(body, [wide_one], [*near_own, v["d2n"]])

    def n1q():
        def body(part1, got0, *refs):
            for p in range(half):
                r = jnp.where(on_odd(), refs[p][0].astype(F32), got0[p].astype(F32))
                refs[-1][p] = (part1[p] + r).astype(BF16)

        d1, = chained(body, [one], [v["part1"], v["got0"], *near_got])
        v["d1n"] = shift(d1, "col", 2)

    def n13():
        n = len(zeros())

        def body(*refs):
            stage1(refs, refs[2 * half:2 * half + n], None if DIRECT_N else refs[-3], refs[-2])
            stage3(refs, refs[-1])

        d1, d3 = chained(body, [one, one], [*near_own, *near_got, *zeros()] + ([] if DIRECT_N else [v["d2n"]]))
        v["d1n"], v["d3n"] = shift(d1, "col", 2), shift(d3, "col", 6)

    def f35():
        def far35(out, more, is_odd, i, part, cut, total):
            r2, r4 = [m[part, :, cut].astype(F32) for m in more]
            if i == 0:
                total = total + jnp.where(is_odd, r4, r2)
            else:
                total = total + jnp.where(is_odd, 0.0, r4)
            out[i][part, :, cut] = total.astype(BF16)

        d2, d3 = products(y[35], (3, 5), far35, [one, one], v["got_far"])
        v["d2f"], v["d3f"] = send2(d2, DIRECT_F), shift(d3, "col", 6)

    def a3n():
        n = len(zeros())

        def body(d3, *refs):
            for p in range(half):
                refs[-1][p] = d3[p].astype(F32) + jnp.where(on_odd(), r0(refs[:n], p), 0.0)

        v["sum_n"], = chained(body, [wide_one], [v["d3n"], *zeros()])

    def a1n():
        ins = [v["d1n"]] + ([v["sum_n"]] if "sum_n" in v else [v["d3n"], *zeros()]) + ([v["d2n"]] if DIRECT_N else [])
        n = len(zeros())

        def body(d1, *refs):
            for p in range(half):
                total = d1[p].astype(F32)
                if "sum_n" in v:
                    total = total + refs[0][p]
                else:
                    total = total + refs[0][p].astype(F32) + jnp.where(on_odd(), r0(refs[1:1 + n], p), 0.0)
                refs[-1][p] = total + refs[-2][p].astype(F32) if DIRECT_N else total

        v["all_n"], = chained(body, [wide_one], ins)

    def f0():
        v["got_last"] = pair_swap(products(y[0], (0,), store, [pinned(1, *strip)], [])[0], "col")

    def f1a():
        v["first"], = products(y[1][0], (1,), plain, [wide_one], [], slice(0, cut_at))

    def a2f():
        ins = [v["got_far"][0]] + ([] if DIRECT_F else [v["d2f"]]) + [v[k] for k in ("first",) if k in v]

        def body(gf, *refs):
            for p in range(half):
                total = jnp.where(on_odd(), gf[p].astype(F32), 0.0)
                for ref in refs[:-1]:
                    total = total + ref[p].astype(F32)
                refs[-1][p] = total

        v["pre"], = chained(body, [wide_one], ins)

    def f1():
        deep = slice(cut_at, depth) if SPLIT else slice(None)
        v["added"] = "pre" in v
        if v["added"]:
            v["raw"], = products(y[1][-1], (1,), added, [wide_one], [v["pre"]], deep)
        else:
            v["raw"], = products(y[1][-1], (1,), plain, [wide_one], [], deep)

    def a3f():
        def body(d3, out):
            out[...] = d3[...].astype(F32)

        v["sum_f"], = chained(body, [wide_one], [v["d3f"]])

    def col():
        early, added = "sum_f" in v, v["added"]

        def collect(total, raw, gl, d3far, *refs):
            sums, lasts = refs[-2 * half:-half], refs[-half:]
            is_odd = on_odd()
            for part in range(half):
                r0 = gl[0, part].astype(F32)
                last = raw[part] + jnp.where(is_odd, 0.0, r0)
                lasts[part][...] = (last if added else last + refs[0][part]).astype(BF16)
                sums[part][0] = total[part]
                sums[part][1] = d3far[part].astype(F32) + jnp.where(is_odd, r0, 0.0)
                if DIRECT_F:
                    sums[part][1] += refs[0 if added else 1][part].astype(F32)

        outs = chained(collect, [pinned(2, quarter, cols, dtype=F32)] * half + [flat] * half,
                       [v["all_n"], v["raw"], v["got_last"], v["sum_f"] if early else v["d3f"]]
                       + ([] if added else [v["pre"]]) + ([v["d2f"]] if DIRECT_F else []))
        sums, v["lasts"] = outs[:half], outs[half:]
        v["sums"] = to_columns(sums, 0)
        v["last_in"] = to_columns(v["lasts"], 2)

    nodes = dict(gy0=gy0, gy1=gy1, gz1=gz1, rest=rest, p0a=p0a, p0b=p0b, p1a=p1a, p1b=p1b, n1p=n1p, n1q=n1q, f24=f24, n2=n2, n3=n3, n23=n23, n1=n1, n13=n13, f35=f35, a3n=a3n, a1n=a1n, f0=f0,
                 f1a=f1a, a2f=a2f, f1=f1, a3f=a3f, col=col)
    for name in ORDER:
        nodes[name]()

    places = [(0, j) for j in range(half)] + [(1, j) for j in range(1, half)] + [(1, 0)]

    def arrange(rhs, diag, _, rhs_out, diag_out):
        me = lax.axis_index("rhs")
        upper, mine = lax.div(me, half), lax.rem(me, half)
        column = lax.broadcasted_iota(jnp.int32, (rows, rows), 1)
        source = column
        for slot, (s, j) in enumerate(places):
            at = slot * quarter
            block = lax.rem(upper + s, 2) * half + lax.rem(mine + half - j, half)
            start = pl.multiple_of(block * quarter, quarter)
            rhs_out[at:at + quarter] = rhs[pl.ds(start, quarter)]
            source = jnp.where((column >= at) & (column < at + quarter), column - at + start, source)
        pick = (lax.broadcasted_iota(jnp.int32, (rows, rows), 0) == source).astype(BF16)
        diag_out[...] = jnp.dot(diag[0], pick, preferred_element_type=F32).astype(BF16)

    rhs_local, diag_local = call(arrange, [pinned(rows, cols), pinned(rows, rows)], [VMEM, VMEM, ANY],
                                 [rhs_block, diag_inverse, near_own[-1]], flops=2 * rows * rows * rows)

    early = rows - quarter
    sums_in, last_in = v["sums"], v["last_in"]

    def most(rhs, diag, *refs):
        acc, last, out = refs[:half], refs[half:2 * half - 1], refs[-1]
        total = jnp.concatenate([a[0] for a in acc] + [a[1] + l[...].astype(F32) for a, l in zip(acc[1:], last)])
        remaining = (rhs[:early].astype(F32) - total).astype(BF16)
        out[...] = jnp.dot(diag[:, :early], remaining, preferred_element_type=F32)

    partial, = call(most, [pinned(rows, cols, dtype=F32)], [VMEM] * (2 + 2 * half - 1) + [ANY],
                    [rhs_local, diag_local, *sums_in, *last_in[1:], v["lasts"][0]], flops=2 * rows * early * cols)

    def final(rhs, diag, acc, last, part, out, block, sems):
        total = acc[1] + last[...].astype(F32)
        remaining = (rhs[early:].astype(F32) - total).astype(BF16)
        copies = []
        for i in range(size):
            cut = slice(i * quarter, (i + 1) * quarter)
            term = jnp.dot(diag[cut, early:], remaining, preferred_element_type=F32)
            block[cut] = (part[cut] + term).astype(BF16)
            copies.append(pltpu.make_async_copy(block.at[cut], out.at[cut], sems.at[i]))
            copies[-1].start()
        for c in copies:
            c.wait()

    return call(final, [jax.ShapeDtypeStruct((rows, cols), BF16)], [VMEM] * 5,
                [rhs_local, diag_local, sums_in[0], last_in[0], partial], flops=2 * rows * quarter * cols,
                out_specs=[ANY], scratch_shapes=[pltpu.VMEM((rows, cols), BF16), pltpu.SemaphoreType.DMA((size,))])[0]

def solution(mesh):
    in_specs = (
        P("col", "rhs"),
        P("col", "rhs"),
        P("col", None, "rhs", None),
        P("col", None),
        P("col", None, None),
    )
    out_specs = P("col", "rhs")
    return jax.shard_map(
        per_device, mesh=mesh, in_specs=in_specs, out_specs=out_specs, check_vma=False
    )
```

```python
import functools

import jax
import jax.numpy as jnp
from jax import lax
from jax.experimental import pallas as pl
from jax.experimental.pallas import tpu as pltpu
from jax.sharding import PartitionSpec as P

F32, BF16 = jnp.float32, jnp.bfloat16
VMEM = pl.BlockSpec(memory_space=pltpu.VMEM)
SMEM = pl.BlockSpec(memory_space=pltpu.SMEM)
ANY = pl.BlockSpec(memory_space=pl.ANY)
HBM = pl.BlockSpec(memory_space=pltpu.HBM)


WIDE = 256
PIECES = 4
SPLIT = 2
FIRST2 = False
DIRECT_N, DIRECT_F = False, False
ORDER = (
    "rest", "p0a", "p0b", "p1a", "p1b", "n2", "f24", "n3", "n1", "a3n",
    "f03", "a1n", "coln", "ff", "a2f", "early", "colf", "fla", "flb",
)


def shift(block, axis, distance):
    size = lax.axis_size(axis)
    return lax.ppermute(block, axis, [(i, (i + distance) % size) for i in range(size)])


def pair_swap(block, axis):
    size = lax.axis_size(axis)
    return lax.ppermute(block, axis, [(i, i ^ 1) for i in range(size)])


def across(block, axis):
    return shift(block, axis, lax.axis_size(axis) // 2)


def inner(i, j, half):
    return i // half * half + (i % half + j) % half


def half_gather(block, axis):
    size = lax.axis_size(axis)
    half = size // 2
    parts = [block]
    for j in range(1, half):
        parts.append(lax.ppermute(block, axis, [(inner(i, j, half), i) for i in range(size)]))
    return parts


def to_columns(blocks, distance):
    n, size = lax.axis_size("col"), lax.axis_size("rhs")
    out = []
    for j, block in enumerate(blocks):
        route = [(c * size + r, (c + distance) % n * size + inner(r, j, size // 2))
                 for c in range(n) for r in range(size)]
        out.append(lax.ppermute(block, ("col", "rhs"), route) if distance or j else block)
    return out


def pinned(*shape, dtype=BF16):
    return pltpu.VMEM(shape, dtype)


def call(body, outs, specs, args, flops=0, space=12, out_specs=None, **more):
    moved = sum(a.size * a.dtype.itemsize for a in args)
    return pl.pallas_call(
        body,
        out_shape=outs,
        in_specs=specs,
        out_specs=out_specs or [VMEM] * len(outs),
        compiler_params=pltpu.CompilerParams(vmem_limit_bytes=space << 20),
        cost_estimate=pl.CostEstimate(flops=flops, bytes_accessed=moved, transcendentals=0),
        **more,
    )(*args)


def take(tiles, groups, *earlier, weights=None):
    n, rows, depth = len(groups), tiles.shape[1], tiles.shape[2]
    extra = [] if weights is None else [SMEM]

    def body(*refs):
        src, dsts, sems = refs[0], refs[-1 - n - len(extra):-1], refs[-1]
        copies = []
        for group, dst in zip(groups, dsts):
            for i, (k, begin, end) in enumerate(group):
                k = tile_of(k, tiles.shape[0])
                columns = pl.ds(begin, end - begin)
                for first in range(0, rows, rows // PIECES):
                    cut = pl.ds(first, rows // PIECES)
                    copies.append(pltpu.make_async_copy(src.at[k, cut, columns], dst.at[i, cut], sems.at[len(copies)]))
        for c in copies:
            c.start()
        if extra:
            for k in range(weights.shape[1]):
                dsts[-1][k:k + 1, :] = jnp.full((1, WIDE), refs[1][0, k].astype(F32))
        for c in copies:
            c.wait()

    outs = [pinned(len(g), rows, g[0][2] - g[0][1]) for g in groups]
    if extra:
        outs.append(pinned(weights.shape[1], WIDE, dtype=F32))
    return call(body, outs, [HBM] + extra + [ANY] * len(earlier),
                [in_hbm(tiles)] + ([] if weights is None else [weights]) + [*earlier], space=2,
                scratch_shapes=[pltpu.SemaphoreType.DMA((PIECES * sum(map(len, groups)),))])


def in_hbm(array):
    return pltpu.with_memory_space_constraint(array, pltpu.HBM)


def on_odd():
    return lax.rem(lax.axis_index("col"), 2) == 1


def on_swap():
    if lax.axis_size("col") % 4:
        return jnp.bool_(False)
    return lax.rem(lax.div(lax.axis_index("col"), 2), 2) == 1


def tile_of(k, hops):
    low, high = (1, hops - 1) if k == "first" else (hops - 1, 1)
    return jnp.where(on_swap(), low, high) if isinstance(k, str) else k


def gate(block, *earlier):
    def body(*refs):
        pass

    return call(body, [jax.ShapeDtypeStruct(block.shape, block.dtype)], [ANY] * (1 + len(earlier)), [block, *earlier],
                space=1, out_specs=[ANY], input_output_aliases={0: 0})[0]


def column_cuts(cols):
    wide = min(WIDE, cols)
    return [slice(at, at + wide) for at in range(0, cols, wide)]


def per_device(rhs_block, solution, factor, tile_list, diag_inverse):
    hops, quarter, depth = factor.shape[1:]
    rows, cols = rhs_block.shape
    size = lax.axis_size("rhs")
    half = size // 2
    tiles = factor[0]
    gives, owns = (2, 4, 0), (3, 5, 1)
    cuts = column_cuts(cols)
    strip = (half, quarter, cols)
    one, wide_one = pinned(*strip), pinned(*strip, dtype=F32)
    flat = pinned(quarter, cols)
    v = {}

    if FIRST2:
        s2, = take(tiles, [[(2, 0, depth)]])
        s4, = take(tiles, [[(4, 0, depth)]], s2)
        s24 = [s2, s4]
    else:
        s24 = list(take(tiles, [[(2, 0, depth), (4, 0, depth)]]))
    y24 = [across(s, "rhs") for s in s24]
    others = half_gather(solution, "rhs")[1:]
    cut_at = depth * SPLIT // 4
    last_tile = [[("last", 0, cut_at)], [("last", cut_at, depth)]] if SPLIT else [[("last", 0, depth)]]
    order = (0, 3, "first", "last")
    sols = [solution, *others]
    v["token"] = s24[-1]

    def chained(body, outs, ins, flops=0):
        n = len(ins)

        def run(*refs):
            body(*refs[:n], *refs[n + 1:])

        got = call(run, outs, [VMEM] * n + [ANY], [*ins, v["token"]], flops=flops)
        v["token"] = got[0]
        return got

    y, taken = {}, []

    def rest():
        groups = [[(0, 0, depth), (3, 0, depth)], [("first", 0, depth)]] + last_tile
        *got, v["weights"] = take(tiles, groups, v["token"], weights=tile_list)
        for name, s in zip(("g03", "gf", "gla", "glb"), got):
            y[name] = s if name in ORDER else across(s, "rhs")
        taken.extend(got)
        v["token"] = got[0]

    def gated(name):
        y[name] = across(gate(y[name], v["token"]), "rhs")

    near_got, near_own, near_give0 = [], [], []

    def near_gives(part):
        def body(*refs):
            lefts, (sol, weights, _, give) = refs[:-4], refs[-4:]
            left = jnp.concatenate([r[i] for r in lefts for i in range(r.shape[0])])
            for cut in cuts:
                total = jnp.dot(left, sol[:, cut], preferred_element_type=F32)
                for i in range(2):
                    term = total[i * quarter:(i + 1) * quarter] * weights[gives[i]:gives[i] + 1, :total.shape[1]]
                    give[i, :, cut] = term.astype(BF16)

        got = call(body, [pinned(2, quarter, cols)], [VMEM] * (len(s24) + 2) + [ANY], [*s24, sols[part], v["weights"], v["token"]],
                   flops=4 * quarter * depth * cols)
        v["token"] = got[0]
        near_got.append(pair_swap(got[0], "col"))

    def near_rest(part):
        n = len(taken)
        joins = half - 1 if part == half - 1 else 0

        def body(*refs):
            lefts, (sol, weights), outs = refs[:n], refs[n:n + 2], refs[n + 3 + joins:]
            whole = [r[i] for r in lefts[:2] for i in range(r.shape[0])]
            left = jnp.concatenate(whole + [jnp.concatenate([r[0] for r in lefts[2:]], axis=1)])
            swap = on_swap()
            for cut in cuts:
                total = jnp.dot(left, sol[:, cut], preferred_element_type=F32)
                zero, three, first, last = [
                    total[at * quarter:(at + 1) * quarter] * weights[pl.ds(tile_of(k, hops), 1), :total.shape[1]]
                    for at, k in enumerate(order)]
                outs[0][0, :, cut] = three
                outs[0][1, :, cut] = jnp.where(swap, last, first)
                outs[0][2, :, cut] = jnp.where(swap, first, last)
                if joins:
                    outs[1][part, :, cut] = zero.astype(BF16)
                else:
                    outs[1][:, cut] = zero.astype(BF16)
            for p in range(joins):
                outs[1][p] = refs[n + 2 + p][...]

        got = call(body, [pinned(3, quarter, cols, dtype=F32), one if joins else flat],
                   [VMEM] * (n + 2 + joins) + [ANY],
                   [*taken, sols[part], v["weights"], *near_give0[:joins], v["token"]],
                   flops=8 * quarter * depth * cols)
        v["token"] = got[0]
        near_own.append(got[0])
        if joins:
            v["got0"] = pair_swap(got[1], "col")
        else:
            near_give0.append(got[1])

    def p0a():
        near_gives(0)

    def p0b():
        near_rest(0)

    def p1a():
        for part in range(1, half):
            near_gives(part)

    def p1b():
        for part in range(1, half):
            near_rest(part)

    def zeros():
        return [v["got0"]]

    def r0(refs, part):
        return refs[0][part].astype(F32)

    def products(far, ks, epilogue, outs, extra, deep=slice(None)):
        n_extra = len(extra)

        far = far if isinstance(far, list) else [far]
        n_far = len(far)

        def body(*refs):
            far_refs, refs = refs[:n_far], refs[n_far:]
            sol_refs, weights = refs[:half], refs[half]
            more = refs[half + 1:half + 1 + n_extra]
            out = refs[len(refs) - len(outs):]
            is_odd = on_odd()
            left = jnp.concatenate([r[i] for r in far_refs for i in range(r.shape[0])])
            for part, sol_ref in enumerate(sol_refs):
                for cut in cuts:
                    total = jnp.dot(left, sol_ref[deep, cut], preferred_element_type=F32)
                    for i, k in enumerate(ks):
                        term = total[i * quarter:(i + 1) * quarter]
                        term = term * weights[pl.ds(tile_of(k, hops), 1), :total.shape[1]]
                        epilogue(out, more, is_odd, i, part, cut, term)

        args = [*far, *sols, v["weights"], *extra, v["token"]]
        specs = [VMEM] * (n_far + half + 1 + n_extra) + [ANY]
        got = call(body, outs, specs, args, flops=2 * len(ks) * quarter * depth * cols * half)
        v["token"] = got[0]
        return got

    def store(out, more, is_odd, i, part, cut, total):
        out[0][i, part, :, cut] = total.astype(BF16)

    def plain(out, more, is_odd, i, part, cut, total):
        out[0][part, :, cut] = total

    def added(out, more, is_odd, i, part, cut, total):
        out[0][part, :, cut] = total + more[0][part, :, cut]

    def f24():
        def each(out, more, is_odd, i, part, cut, total):
            out[i][part, :, cut] = total.astype(BF16)

        v["got_far"] = [pair_swap(g, "col") for g in products(y24, (2, 4), each, [one, one], [])]

    def stage2(refs, d2):
        for p in range(half):
            own, got = refs[p], refs[half + p]
            d2[p] = (own[0] + jnp.where(on_odd(), got[1].astype(F32), got[0].astype(F32))).astype(BF16)

    def stage3(refs, d3):
        for p in range(half):
            own, got = refs[p], refs[half + p]
            d3[p] = (own[1] + jnp.where(on_odd(), 0.0, got[1].astype(F32))).astype(BF16)

    def stage1(refs, others, arrived, d1):
        for p in range(half):
            own, got = refs[p], refs[half + p]
            r = jnp.where(on_odd(), got[0].astype(F32), r0(others, p))
            total = own[2] + r
            d1[p] = (total if arrived is None else total + arrived[p].astype(F32)).astype(BF16)

    def send2(total, direct):
        return shift(total, "col", 4 if direct else 2)

    def n2():
        d2, = chained(lambda *refs: stage2(refs, refs[-1]), [one], [*near_own, *near_got])
        v["d2n"] = send2(d2, DIRECT_N)

    def n3():
        d3, = chained(lambda *refs: stage3(refs, refs[-1]), [one], [*near_own, *near_got])
        v["d3n"] = shift(d3, "col", 6)

    def n23():
        def body(*refs):
            stage2(refs, refs[-2])
            stage3(refs, refs[-1])

        d2, d3 = chained(body, [one, one], [*near_own, *near_got])
        v["d2n"], v["d3n"] = send2(d2, DIRECT_N), shift(d3, "col", 6)

    def n1():
        n = len(zeros())
        d1, = chained(lambda *refs: stage1(refs, refs[2 * half:2 * half + n], None if DIRECT_N else refs[-2], refs[-1]),
                      [one], [*near_own, *near_got, *zeros()] + ([] if DIRECT_N else [v["d2n"]]))
        v["d1n"] = shift(d1, "col", 2)

    def n1p():
        def body(*refs):
            for p in range(half):
                refs[-1][p] = refs[p][2] + refs[half][p].astype(F32)

        v["part1"], = chained(body, [wide_one], [*near_own, v["d2n"]])

    def n1q():
        def body(part1, got0, *refs):
            for p in range(half):
                r = jnp.where(on_odd(), refs[p][0].astype(F32), got0[p].astype(F32))
                refs[-1][p] = (part1[p] + r).astype(BF16)

        d1, = chained(body, [one], [v["part1"], v["got0"], *near_got])
        v["d1n"] = shift(d1, "col", 2)

    def n13():
        n = len(zeros())

        def body(*refs):
            stage1(refs, refs[2 * half:2 * half + n], None if DIRECT_N else refs[-3], refs[-2])
            stage3(refs, refs[-1])

        d1, d3 = chained(body, [one, one], [*near_own, *near_got, *zeros()] + ([] if DIRECT_N else [v["d2n"]]))
        v["d1n"], v["d3n"] = shift(d1, "col", 2), shift(d3, "col", 6)

    def f03():
        def far03(out, more, is_odd, i, part, cut, total):
            r2, r4 = [m[part, :, cut].astype(F32) for m in more]
            if i == 1:
                total = total + jnp.where(is_odd, r4, r2)
            out[i][part, :, cut] = total.astype(BF16)

        give, d2 = products(y["g03"], (0, 3), far03, [one, one], v["got_far"])
        v["got_last"], v["d2f"] = pair_swap(give, "col"), shift(d2, "col", 2)

    def a3n():
        n = len(zeros())

        def body(d3, *refs):
            for p in range(half):
                refs[-1][p] = d3[p].astype(F32) + jnp.where(on_odd(), r0(refs[:n], p), 0.0)

        v["sum_n"], = chained(body, [wide_one], [v["d3n"], *zeros()])

    def a1n():
        ins = [v["d1n"]] + ([v["sum_n"]] if "sum_n" in v else [v["d3n"], *zeros()]) + ([v["d2n"]] if DIRECT_N else [])
        n = len(zeros())

        def body(d1, *refs):
            for p in range(half):
                total = d1[p].astype(F32)
                if "sum_n" in v:
                    total = total + refs[0][p]
                else:
                    total = total + refs[0][p].astype(F32) + jnp.where(on_odd(), r0(refs[1:1 + n], p), 0.0)
                refs[-1][p] = total + refs[-2][p].astype(F32) if DIRECT_N else total

        v["all_n"], = chained(body, [wide_one], ins)

    def ff():
        v["raw_f"], = products(y["gf"], ("first",), plain, [wide_one], [])

    def send(parts, last):
        n = lax.axis_size("col")
        swaps = [n % 4 == 0 and c // 2 % 2 == 1 for c in range(n)]
        far_off = [c + (2 if last != swap else hops) for c, swap in enumerate(swaps)]
        out = []
        for j, part in enumerate(parts):
            route = [(c * size + r, far_off[c] % n * size + inner(r, j, half)) for c in range(n) for r in range(size)]
            out.append(lax.ppermute(part, ("col", "rhs"), route))
        return out

    def a2f():
        def body(d2, r2, out):
            for p in range(half):
                out[p] = d2[p].astype(F32) + jnp.where(on_odd(), r2[p].astype(F32), 0.0)

        v["pre2"], = chained(body, [wide_one], [v["d2f"], v["got_far"][0]])

    def early():
        def body(raw, r4, r0, pre2, *refs):
            outs, pre = refs[:half], refs[half]
            is_odd, swap = on_odd(), on_swap()
            for p in range(half):
                one = pre2[p] + jnp.where(is_odd, 0.0, r0[p].astype(F32))
                three = jnp.where(is_odd, 0.0, r4[p].astype(F32))
                outs[p][...] = (raw[p] + jnp.where(swap, one, three)).astype(BF16)
                pre[p] = jnp.where(swap, three, one)

        *outs, v["pre"] = chained(body, [flat] * half + [wide_one],
                                  [v["raw_f"], v["got_far"][1], v["got_last"], v["pre2"]])
        v["early_in"] = send(outs, False)

    def coln():
        def body(total, *outs):
            for part in range(half):
                outs[part][...] = total[part]

        v["sums_n"] = to_columns(chained(body, [pinned(quarter, cols, dtype=F32)] * half, [v["all_n"]]), 0)

    def colf():
        def body(r0, *outs):
            for part in range(half):
                outs[part][...] = jnp.where(on_odd(), r0[part].astype(F32), 0.0).astype(BF16)

        v["sums_f"] = to_columns(chained(body, [flat] * half, [v["got_last"]]), 0)

    def fla():
        v["first"], = products(y["gla"], ("last",), plain, [wide_one], [], slice(0, cut_at))

    def flb():
        def added(out, more, is_odd, i, part, cut, total):
            for m in more:
                total = total + m[part, :, cut]
            out[part][:, cut] = total.astype(BF16)

        if SPLIT:
            v["lasts"] = products(y["glb"], ("last",), added, [flat] * half, [v["first"], v["pre"]], slice(cut_at, depth))
        else:
            v["lasts"] = products(y["gla"], ("last",), added, [flat] * half, [v["pre"]])
        v["last_in"] = send(v["lasts"], True)

    nodes = dict(rest=rest, p0a=p0a, p0b=p0b, p1a=p1a, p1b=p1b, f24=f24, n2=n2, n3=n3, n23=n23, n1=n1, f03=f03, a3n=a3n,
                 a1n=a1n, ff=ff, a2f=a2f, early=early, coln=coln, colf=colf, fla=fla, flb=flb)
    for name in ORDER:
        if name in y:
            gated(name)
        else:
            nodes[name]()

    places = [(0, j) for j in range(half)] + [(1, j) for j in range(1, half)] + [(1, 0)]

    def arrange(rhs, diag, _, rhs_out, diag_out):
        me = lax.axis_index("rhs")
        upper, mine = lax.div(me, half), lax.rem(me, half)
        column = lax.broadcasted_iota(jnp.int32, (rows, rows), 1)
        source = column
        for slot, (s, j) in enumerate(places):
            at = slot * quarter
            block = lax.rem(upper + s, 2) * half + lax.rem(mine + half - j, half)
            start = pl.multiple_of(block * quarter, quarter)
            rhs_out[at:at + quarter] = rhs[pl.ds(start, quarter)]
            source = jnp.where((column >= at) & (column < at + quarter), column - at + start, source)
        pick = (lax.broadcasted_iota(jnp.int32, (rows, rows), 0) == source).astype(BF16)
        diag_out[...] = jnp.dot(diag[0], pick, preferred_element_type=F32).astype(BF16)

    rhs_local, diag_local = call(arrange, [pinned(rows, cols), pinned(rows, rows)], [VMEM, VMEM, ANY],
                                 [rhs_block, diag_inverse, near_own[-1]], flops=2 * rows * rows * rows)

    most_rows = rows - quarter
    early_in, last_in = v["early_in"], v["last_in"]

    def gather(*refs):
        near, stay, far, out = refs[:half], refs[half:2 * half], refs[2 * half:3 * half], refs[-1]
        for j in range(half):
            out[j * quarter:(j + 1) * quarter] = near[j][...]
        for j in range(half):
            at = (half + (j - 1) % half) * quarter
            out[at:at + quarter] = stay[j][...].astype(F32) + far[j][...].astype(F32)

    known, = chained(gather, [pinned(rows, cols, dtype=F32)], [*v["sums_n"], *v["sums_f"], *early_in])

    def most(rhs, diag, known, *refs):
        last, out = refs[:half - 1], refs[-1]
        total = jnp.concatenate([known[:rows // 2]] + [known[(half + j) * quarter:(half + j + 1) * quarter]
                                                      + l[...].astype(F32) for j, l in enumerate(last)])
        remaining = (rhs[:most_rows].astype(F32) - total).astype(BF16)
        out[...] = jnp.dot(diag[:, :most_rows], remaining, preferred_element_type=F32)

    partial, = chained(most, [pinned(rows, cols, dtype=F32)], [rhs_local, diag_local, known, *last_in[1:]],
                       flops=2 * rows * most_rows * cols)

    def final(rhs, diag, known, last, part, out, block, sems):
        total = known[most_rows:] + last[...].astype(F32)
        remaining = (rhs[most_rows:].astype(F32) - total).astype(BF16)
        copies = []
        for i in range(size):
            cut = slice(i * quarter, (i + 1) * quarter)
            term = jnp.dot(diag[cut, most_rows:], remaining, preferred_element_type=F32)
            block[cut] = (part[cut] + term).astype(BF16)
            copies.append(pltpu.make_async_copy(block.at[cut], out.at[cut], sems.at[i]))
            copies[-1].start()
        for c in copies:
            c.wait()

    return call(final, [jax.ShapeDtypeStruct((rows, cols), BF16)], [VMEM] * 5,
                [rhs_local, diag_local, known, last_in[0], partial], flops=2 * rows * quarter * cols,
                out_specs=[ANY], scratch_shapes=[pltpu.VMEM((rows, cols), BF16), pltpu.SemaphoreType.DMA((size,))])[0]

def solution(mesh):
    in_specs = (
        P("col", "rhs"),
        P("col", "rhs"),
        P("col", None, "rhs", None),
        P("col", None),
        P("col", None, None),
    )
    out_specs = P("col", "rhs")
    return jax.shard_map(
        per_device, mesh=mesh, in_specs=in_specs, out_specs=out_specs, check_vma=False
    )
```

```python
import functools

import jax
import jax.numpy as jnp
from jax import lax
from jax.experimental import pallas as pl
from jax.experimental.pallas import tpu as pltpu
from jax.sharding import PartitionSpec as P

F32, BF16 = jnp.float32, jnp.bfloat16
VMEM = pl.BlockSpec(memory_space=pltpu.VMEM)
SMEM = pl.BlockSpec(memory_space=pltpu.SMEM)
ANY = pl.BlockSpec(memory_space=pl.ANY)
HBM = pl.BlockSpec(memory_space=pltpu.HBM)


WIDE = 256
PIECES = 4


def shift(block, axis, distance):
    size = lax.axis_size(axis)
    return lax.ppermute(block, axis, [(i, (i + distance) % size) for i in range(size)])


def pair_swap(block, axis):
    size = lax.axis_size(axis)
    return lax.ppermute(block, axis, [(i, i ^ 1) for i in range(size)])


def across(block, axis):
    return shift(block, axis, lax.axis_size(axis) // 2)


def inner(i, j, half):
    return i // half * half + (i % half + j) % half


def half_gather(block, axis):
    size = lax.axis_size(axis)
    half = size // 2
    parts = [block]
    for j in range(1, half):
        parts.append(lax.ppermute(block, axis, [(inner(i, j, half), i) for i in range(size)]))
    return parts


def to_columns(blocks, distance):
    n, size = lax.axis_size("col"), lax.axis_size("rhs")
    out = []
    for j, block in enumerate(blocks):
        route = [(c * size + r, (c + distance) % n * size + inner(r, j, size // 2))
                 for c in range(n) for r in range(size)]
        out.append(lax.ppermute(block, ("col", "rhs"), route) if distance or j else block)
    return out


def pinned(*shape, dtype=BF16):
    return pltpu.VMEM(shape, dtype)


def call(body, outs, specs, args, flops=0, space=12, out_specs=None, **more):
    moved = sum(a.size * a.dtype.itemsize for a in args)
    return pl.pallas_call(
        body,
        out_shape=outs,
        in_specs=specs,
        out_specs=out_specs or [VMEM] * len(outs),
        compiler_params=pltpu.CompilerParams(vmem_limit_bytes=space << 20),
        cost_estimate=pl.CostEstimate(flops=flops, bytes_accessed=moved, transcendentals=0),
        **more,
    )(*args)


def take(tiles, groups, *earlier, weights=None):
    n, rows, depth = len(groups), tiles.shape[1], tiles.shape[2]
    extra = [] if weights is None else [SMEM]

    def body(*refs):
        src, dsts, sems = refs[0], refs[-1 - n - len(extra):-1], refs[-1]
        copies = []
        for group, dst in zip(groups, dsts):
            for i, (k, begin, end) in enumerate(group):
                k = tile_of(k, tiles.shape[0])
                columns = pl.ds(begin, end - begin)
                for first in range(0, rows, rows // PIECES):
                    cut = pl.ds(first, rows // PIECES)
                    copies.append(pltpu.make_async_copy(src.at[k, cut, columns], dst.at[i, cut], sems.at[len(copies)]))
        for c in copies:
            c.start()
        if extra:
            for k in range(weights.shape[1]):
                dsts[-1][k:k + 1, :] = jnp.full((1, WIDE), refs[1][0, k].astype(F32))
        for c in copies:
            c.wait()

    outs = [pinned(len(g), rows, g[0][2] - g[0][1]) for g in groups]
    if extra:
        outs.append(pinned(weights.shape[1], WIDE, dtype=F32))
    return call(body, outs, [HBM] + extra + [ANY] * len(earlier),
                [in_hbm(tiles)] + ([] if weights is None else [weights]) + [*earlier], space=2,
                scratch_shapes=[pltpu.SemaphoreType.DMA((PIECES * sum(map(len, groups)),))])


def in_hbm(array):
    return pltpu.with_memory_space_constraint(array, pltpu.HBM)


def on_odd():
    return lax.rem(lax.axis_index("col"), 2) == 1


def on_swap():
    if lax.axis_size("col") % 4:
        return jnp.bool_(False)
    return lax.rem(lax.div(lax.axis_index("col"), 2), 2) == 1


def tile_of(k, hops):
    low, high = (1, hops - 1) if k == "first" else (hops - 1, 1)
    return jnp.where(on_swap(), low, high) if isinstance(k, str) else k


def column_cuts(cols):
    wide = min(WIDE, cols)
    return [slice(at, at + wide) for at in range(0, cols, wide)]


def per_device(rhs_block, solution, factor, tile_list, diag_inverse):
    hops, quarter, depth = factor.shape[1:]
    rows, cols = rhs_block.shape
    size = lax.axis_size("rhs")
    half = size // 2
    tiles = factor[0]
    gives, owns = (2, 4, 0), (3, 5, 1)
    cuts = column_cuts(cols)
    strip = (half, quarter, cols)
    one, wide_one = pinned(*strip), pinned(*strip, dtype=F32)
    flat = pinned(quarter, cols)
    v = {}

    s24, = take(tiles, [[(2, 0, depth), (4, 0, depth)]])
    y24 = across(s24, "rhs")
    others = half_gather(solution, "rhs")[1:]
    middle = depth // 2
    sols = [solution, *others]
    v["token"] = s24

    def chained(body, outs, ins, flops=0):
        n = len(ins)

        def run(*refs):
            body(*refs[:n], *refs[n + 1:])

        got = call(run, outs, [VMEM] * n + [ANY], [*ins, v["token"]], flops=flops)
        v["token"] = got[0]
        return got

    order = (0, 3, "first", "last")
    groups = [[(0, 0, depth), (3, 0, depth)], [("first", 0, depth)], [("last", 0, middle)], [("last", middle, depth)]]
    *taken, v["weights"] = take(tiles, groups, s24, weights=tile_list)
    y03, y_first, y_last, y_last_rest = [across(s, "rhs") for s in taken]
    v["token"] = taken[0]

    near_got, near_own, near_give0 = [], [], []

    def near_gives(part):
        def body(*refs):
            left_ref, sol, weights, _, give = refs
            left = left_ref[...].reshape(2 * quarter, depth)
            for cut in cuts:
                total = jnp.dot(left, sol[:, cut], preferred_element_type=F32)
                for i in range(2):
                    term = total[i * quarter:(i + 1) * quarter] * weights[gives[i]:gives[i] + 1, :total.shape[1]]
                    give[i, :, cut] = term.astype(BF16)

        got = call(body, [pinned(2, quarter, cols)], [VMEM] * 3 + [ANY],
                   [s24, sols[part], v["weights"], v["token"]], flops=4 * quarter * depth * cols)
        v["token"] = got[0]
        near_got.append(pair_swap(got[0], "col"))

    def near_rest(part):
        n = len(taken)
        joins = half - 1 if part == half - 1 else 0

        def body(*refs):
            lefts, (sol, weights), outs = refs[:n], refs[n:n + 2], refs[n + 3 + joins:]
            whole = [r[i] for r in lefts[:2] for i in range(r.shape[0])]
            left = jnp.concatenate(whole + [jnp.concatenate([r[0] for r in lefts[2:]], axis=1)])
            swap = on_swap()
            for cut in cuts:
                total = jnp.dot(left, sol[:, cut], preferred_element_type=F32)
                zero, three, first, last = [
                    total[at * quarter:(at + 1) * quarter] * weights[pl.ds(tile_of(k, hops), 1), :total.shape[1]]
                    for at, k in enumerate(order)]
                outs[0][0, :, cut] = three
                outs[0][1, :, cut] = jnp.where(swap, last, first)
                outs[0][2, :, cut] = jnp.where(swap, first, last)
                if joins:
                    outs[1][part, :, cut] = zero.astype(BF16)
                else:
                    outs[1][:, cut] = zero.astype(BF16)
            for p in range(joins):
                outs[1][p] = refs[n + 2 + p][...]

        got = call(body, [pinned(3, quarter, cols, dtype=F32), one if joins else flat],
                   [VMEM] * (n + 2 + joins) + [ANY],
                   [*taken, sols[part], v["weights"], *near_give0[:joins], v["token"]],
                   flops=8 * quarter * depth * cols)
        v["token"] = got[0]
        near_own.append(got[0])
        if joins:
            v["got0"] = pair_swap(got[1], "col")
        else:
            near_give0.append(got[1])

    for part in range(half):
        near_gives(part)
        near_rest(part)

    def products(far, ks, epilogue, outs, extra, deep=slice(None)):
        n_extra = len(extra)

        def body(*refs):
            far_ref, refs = refs[0], refs[1:]
            sol_refs, weights = refs[:half], refs[half]
            more = refs[half + 1:half + 1 + n_extra]
            out = refs[len(refs) - len(outs):]
            is_odd = on_odd()
            left = far_ref[...].reshape(len(ks) * quarter, far_ref.shape[2])
            for part, sol_ref in enumerate(sol_refs):
                for cut in cuts:
                    total = jnp.dot(left, sol_ref[deep, cut], preferred_element_type=F32)
                    for i, k in enumerate(ks):
                        term = total[i * quarter:(i + 1) * quarter]
                        term = term * weights[pl.ds(tile_of(k, hops), 1), :total.shape[1]]
                        epilogue(out, more, is_odd, i, part, cut, term)

        args = [far, *sols, v["weights"], *extra, v["token"]]
        specs = [VMEM] * (half + 2 + n_extra) + [ANY]
        got = call(body, outs, specs, args, flops=2 * len(ks) * quarter * depth * cols * half)
        v["token"] = got[0]
        return got

    def plain(out, more, is_odd, i, part, cut, total):
        out[0][part, :, cut] = total

    def rounded(out, more, is_odd, i, part, cut, total):
        out[i][part, :, cut] = total.astype(BF16)


    def near2(*refs):
        for p in range(half):
            own, got = refs[p], refs[half + p]
            refs[-1][p] = (own[0] + jnp.where(on_odd(), got[1].astype(F32), got[0].astype(F32))).astype(BF16)

    d2n, = chained(near2, [one], [*near_own, *near_got])
    d2n_in = shift(d2n, "col", 2)

    got_far = [pair_swap(g, "col") for g in products(y24, (2, 4), rounded, [one, one], [])]

    def near3(*refs):
        for p in range(half):
            own, got = refs[p], refs[half + p]
            refs[-1][p] = (own[1] + jnp.where(on_odd(), 0.0, got[1].astype(F32))).astype(BF16)

    d3n, = chained(near3, [one], [*near_own, *near_got])
    d3n_in = shift(d3n, "col", hops)

    def near1(*refs):
        got0, arrived, d1 = refs[2 * half:]
        for p in range(half):
            own, got = refs[p], refs[half + p]
            r = jnp.where(on_odd(), got[0].astype(F32), got0[p].astype(F32))
            d1[p] = (own[2] + r + arrived[p].astype(F32)).astype(BF16)

    d1n, = chained(near1, [one], [*near_own, *near_got, v["got0"], d2n_in])
    d1n_in = shift(d1n, "col", 2)

    def near3_in(d3, got0, out):
        for p in range(half):
            out[p] = d3[p].astype(F32) + jnp.where(on_odd(), got0[p].astype(F32), 0.0)

    near_sum, = chained(near3_in, [wide_one], [d3n_in, v["got0"]])

    def far03(out, more, is_odd, i, part, cut, total):
        r2, r4 = [m[part, :, cut].astype(F32) for m in more]
        if i == 1:
            total = total + jnp.where(is_odd, r4, r2)
        out[i][part, :, cut] = total.astype(BF16)

    last_give, d2f = products(y03, (0, 3), far03, [one, one], got_far)
    got_last, d2f_in = pair_swap(last_give, "col"), shift(d2f, "col", 2)

    def near1_in(d1, sums, *outs):
        for p in range(half):
            outs[p][...] = d1[p].astype(F32) + sums[p]

    sums_n = chained(near1_in, [pinned(quarter, cols, dtype=F32)] * half, [d1n_in, near_sum])
    sums_n = to_columns(sums_n, 0)

    raw, = products(y_first, ("first",), plain, [wide_one], [])

    def send(parts, last):
        n = lax.axis_size("col")
        swaps = [n % 4 == 0 and c // 2 % 2 == 1 for c in range(n)]
        far_off = [c + (2 if last != swap else hops) for c, swap in enumerate(swaps)]
        out = []
        for j, part in enumerate(parts):
            route = [(c * size + r, far_off[c] % n * size + inner(r, j, half)) for c in range(n) for r in range(size)]
            out.append(lax.ppermute(part, ("col", "rhs"), route))
        return out

    def far2_in(d2, r2, out):
        for p in range(half):
            out[p] = d2[p].astype(F32) + jnp.where(on_odd(), r2[p].astype(F32), 0.0)

    chain, = chained(far2_in, [wide_one], [d2f_in, got_far[0]])

    def far_first(raw, r4, r0, chain, *refs):
        outs, pre = refs[:half], refs[half]
        is_odd, swap = on_odd(), on_swap()
        for p in range(half):
            one = chain[p] + jnp.where(is_odd, 0.0, r0[p].astype(F32))
            three = jnp.where(is_odd, 0.0, r4[p].astype(F32))
            outs[p][...] = (raw[p] + jnp.where(swap, one, three)).astype(BF16)
            pre[p] = jnp.where(swap, three, one)

    *firsts, pre = chained(far_first, [flat] * half + [wide_one], [raw, got_far[1], got_last, chain])
    first_in = send(firsts, False)

    def far_stay(r0, *outs):
        for p in range(half):
            outs[p][...] = jnp.where(on_odd(), r0[p].astype(F32), 0.0).astype(BF16)

    sums_f = to_columns(chained(far_stay, [flat] * half, [got_last]), 0)

    part1, = products(y_last, ("last",), plain, [wide_one], [], slice(0, middle))

    def added(out, more, is_odd, i, part, cut, total):
        for m in more:
            total = total + m[part, :, cut]
        out[part][:, cut] = total.astype(BF16)

    lasts = products(y_last_rest, ("last",), added, [flat] * half, [part1, pre], slice(middle, depth))
    last_in = send(lasts, True)

    places = [(0, j) for j in range(half)] + [(1, j) for j in range(1, half)] + [(1, 0)]

    def arrange(rhs, diag, _, rhs_out, diag_out):
        me = lax.axis_index("rhs")
        upper, mine = lax.div(me, half), lax.rem(me, half)
        column = lax.broadcasted_iota(jnp.int32, (rows, rows), 1)
        source = column
        for slot, (s, j) in enumerate(places):
            at = slot * quarter
            block = lax.rem(upper + s, 2) * half + lax.rem(mine + half - j, half)
            start = pl.multiple_of(block * quarter, quarter)
            rhs_out[at:at + quarter] = rhs[pl.ds(start, quarter)]
            source = jnp.where((column >= at) & (column < at + quarter), column - at + start, source)
        pick = (lax.broadcasted_iota(jnp.int32, (rows, rows), 0) == source).astype(BF16)
        diag_out[...] = jnp.dot(diag[0], pick, preferred_element_type=F32).astype(BF16)

    rhs_local, diag_local = call(arrange, [pinned(rows, cols), pinned(rows, rows)], [VMEM, VMEM, ANY],
                                 [rhs_block, diag_inverse, near_own[-1]], flops=2 * rows * rows * rows)

    most_rows = rows - quarter

    def gather(*refs):
        near, stay, far, out = refs[:half], refs[half:2 * half], refs[2 * half:3 * half], refs[-1]
        for j in range(half):
            out[j * quarter:(j + 1) * quarter] = near[j][...]
        for j in range(half):
            at = (half + (j - 1) % half) * quarter
            out[at:at + quarter] = stay[j][...].astype(F32) + far[j][...].astype(F32)

    known, = chained(gather, [pinned(rows, cols, dtype=F32)], [*sums_n, *sums_f, *first_in])

    def most(rhs, diag, known, *refs):
        last, out = refs[:half - 1], refs[-1]
        total = jnp.concatenate([known[:rows // 2]] + [known[(half + j) * quarter:(half + j + 1) * quarter]
                                                      + l[...].astype(F32) for j, l in enumerate(last)])
        remaining = (rhs[:most_rows].astype(F32) - total).astype(BF16)
        out[...] = jnp.dot(diag[:, :most_rows], remaining, preferred_element_type=F32)

    partial, = chained(most, [pinned(rows, cols, dtype=F32)], [rhs_local, diag_local, known, *last_in[1:]],
                       flops=2 * rows * most_rows * cols)

    def final(rhs, diag, known, last, part, out, block, sems):
        total = known[most_rows:] + last[...].astype(F32)
        remaining = (rhs[most_rows:].astype(F32) - total).astype(BF16)
        copies = []
        for i in range(size):
            cut = slice(i * quarter, (i + 1) * quarter)
            term = jnp.dot(diag[cut, most_rows:], remaining, preferred_element_type=F32)
            block[cut] = (part[cut] + term).astype(BF16)
            copies.append(pltpu.make_async_copy(block.at[cut], out.at[cut], sems.at[i]))
            copies[-1].start()
        for c in copies:
            c.wait()

    return call(final, [jax.ShapeDtypeStruct((rows, cols), BF16)], [VMEM] * 5,
                [rhs_local, diag_local, known, last_in[0], partial], flops=2 * rows * quarter * cols,
                out_specs=[ANY], scratch_shapes=[pltpu.VMEM((rows, cols), BF16), pltpu.SemaphoreType.DMA((size,))])[0]


def solution(mesh):
    in_specs = (
        P("col", "rhs"),
        P("col", "rhs"),
        P("col", None, "rhs", None),
        P("col", None),
        P("col", None, None),
    )
    out_specs = P("col", "rhs")
    return jax.shard_map(
        per_device, mesh=mesh, in_specs=in_specs, out_specs=out_specs, check_vma=False
    )
```

```python
import functools

import jax
import jax.numpy as jnp
from jax import lax
from jax.experimental import pallas as pl
from jax.experimental.pallas import tpu as pltpu
from jax.sharding import PartitionSpec as P

F32, BF16 = jnp.float32, jnp.bfloat16
VMEM = pl.BlockSpec(memory_space=pltpu.VMEM)
SMEM = pl.BlockSpec(memory_space=pltpu.SMEM)
ANY = pl.BlockSpec(memory_space=pl.ANY)
HBM = pl.BlockSpec(memory_space=pltpu.HBM)


WIDE = 256
PIECES = 4


def shift(block, axis, distance):
    size = lax.axis_size(axis)
    return lax.ppermute(block, axis, [(i, (i + distance) % size) for i in range(size)])


def pair_swap(block, axis):
    size = lax.axis_size(axis)
    return lax.ppermute(block, axis, [(i, i ^ 1) for i in range(size)])


def across(block, axis):
    return shift(block, axis, lax.axis_size(axis) // 2)


def inner(i, j, half):
    return i // half * half + (i % half + j) % half


def half_gather(block, axis):
    size = lax.axis_size(axis)
    half = size // 2
    parts = [block]
    for j in range(1, half):
        parts.append(lax.ppermute(block, axis, [(inner(i, j, half), i) for i in range(size)]))
    return parts


def to_columns(blocks, distance):
    n, size = lax.axis_size("col"), lax.axis_size("rhs")
    out = []
    for j, block in enumerate(blocks):
        route = [(c * size + r, (c + distance) % n * size + inner(r, j, size // 2))
                 for c in range(n) for r in range(size)]
        out.append(lax.ppermute(block, ("col", "rhs"), route) if distance or j else block)
    return out


def pinned(*shape, dtype=BF16):
    return pltpu.VMEM(shape, dtype)


def call(body, outs, specs, args, flops=0, space=12, out_specs=None, **more):
    moved = sum(a.size * a.dtype.itemsize for a in args)
    return pl.pallas_call(
        body,
        out_shape=outs,
        in_specs=specs,
        out_specs=out_specs or [VMEM] * len(outs),
        compiler_params=pltpu.CompilerParams(vmem_limit_bytes=space << 20),
        cost_estimate=pl.CostEstimate(flops=flops, bytes_accessed=moved, transcendentals=0),
        **more,
    )(*args)


def take(tiles, groups, *earlier, weights=None):
    n, rows, depth = len(groups), tiles.shape[1], tiles.shape[2]
    extra = [] if weights is None else [SMEM]

    def body(*refs):
        src, dsts, sems = refs[0], refs[-1 - n - len(extra):-1], refs[-1]
        copies = []
        for group, dst in zip(groups, dsts):
            for i, (k, begin, end) in enumerate(group):
                k = tile_of(k, tiles.shape[0])
                columns = pl.ds(begin, end - begin)
                for first in range(0, rows, rows // PIECES):
                    cut = pl.ds(first, rows // PIECES)
                    copies.append(pltpu.make_async_copy(src.at[k, cut, columns], dst.at[i, cut], sems.at[len(copies)]))
        for c in copies:
            c.start()
        if extra:
            for k in range(weights.shape[1]):
                dsts[-1][k:k + 1, :] = jnp.full((1, WIDE), refs[1][0, k].astype(F32))
        for c in copies:
            c.wait()

    outs = [pinned(len(g), rows, g[0][2] - g[0][1]) for g in groups]
    if extra:
        outs.append(pinned(weights.shape[1], WIDE, dtype=F32))
    return call(body, outs, [HBM] + extra + [ANY] * len(earlier),
                [in_hbm(tiles)] + ([] if weights is None else [weights]) + [*earlier], space=2,
                scratch_shapes=[pltpu.SemaphoreType.DMA((PIECES * sum(map(len, groups)),))])


def in_hbm(array):
    return pltpu.with_memory_space_constraint(array, pltpu.HBM)


def on_odd():
    return lax.rem(lax.axis_index("col"), 2) == 1


def on_swap():
    if lax.axis_size("col") % 4:
        return jnp.bool_(False)
    return lax.rem(lax.div(lax.axis_index("col"), 2), 2) == 1


def tile_of(k, hops):
    low, high = (1, hops - 1) if k == "first" else (hops - 1, 1)
    return jnp.where(on_swap(), low, high) if isinstance(k, str) else k


def column_cuts(cols):
    wide = min(WIDE, cols)
    return [slice(at, at + wide) for at in range(0, cols, wide)]


def per_device(rhs_block, solution, factor, tile_list, diag_inverse):
    hops, quarter, depth = factor.shape[1:]
    rows, cols = rhs_block.shape
    size = lax.axis_size("rhs")
    half = size // 2
    tiles = factor[0]
    gives, owns = (2, 4, 0), (3, 5, 1)
    cuts = column_cuts(cols)
    strip = (half, quarter, cols)
    one, wide_one = pinned(*strip), pinned(*strip, dtype=F32)
    flat = pinned(quarter, cols)
    v = {}

    s24, = take(tiles, [[(2, 0, depth), (4, 0, depth)]])
    y24 = across(s24, "rhs")
    others = half_gather(solution, "rhs")[1:]
    middle = depth // 2
    sols = [solution, *others]
    v["token"] = s24

    def chained(body, outs, ins, flops=0):
        n = len(ins)

        def run(*refs):
            body(*refs[:n], *refs[n + 1:])

        got = call(run, outs, [VMEM] * n + [ANY], [*ins, v["token"]], flops=flops)
        v["token"] = got[0]
        return got

    order = (0, 3, "first", "last")
    groups = [[(0, 0, depth), (3, 0, depth)], [("first", 0, depth)], [("last", 0, middle)], [("last", middle, depth)]]
    *taken, v["weights"] = take(tiles, groups, s24, weights=tile_list)
    y03, y_first, y_last, y_last_rest = [across(s, "rhs") for s in taken]
    v["token"] = taken[0]

    near_got, near_own, near_give0 = [], [], []

    def near_gives(part):
        def body(*refs):
            left_ref, sol, weights, _, give = refs
            left = left_ref[...].reshape(2 * quarter, depth)
            for cut in cuts:
                total = jnp.dot(left, sol[:, cut], preferred_element_type=F32)
                for i in range(2):
                    term = total[i * quarter:(i + 1) * quarter] * weights[gives[i]:gives[i] + 1, :total.shape[1]]
                    give[i, :, cut] = term.astype(BF16)

        got = call(body, [pinned(2, quarter, cols)], [VMEM] * 3 + [ANY],
                   [s24, sols[part], v["weights"], v["token"]], flops=4 * quarter * depth * cols)
        v["token"] = got[0]
        near_got.append(pair_swap(got[0], "col"))

    def near_rest(part):
        n = len(taken)
        joins = half - 1 if part == half - 1 else 0

        def body(*refs):
            lefts, (sol, weights), outs = refs[:n], refs[n:n + 2], refs[n + 3 + joins:]
            whole = [r[i] for r in lefts[:2] for i in range(r.shape[0])]
            left = jnp.concatenate(whole + [jnp.concatenate([r[0] for r in lefts[2:]], axis=1)])
            swap = on_swap()
            for cut in cuts:
                total = jnp.dot(left, sol[:, cut], preferred_element_type=F32)
                zero, three, first, last = [
                    total[at * quarter:(at + 1) * quarter] * weights[pl.ds(tile_of(k, hops), 1), :total.shape[1]]
                    for at, k in enumerate(order)]
                outs[0][0, :, cut] = three
                outs[0][1, :, cut] = jnp.where(swap, last, first)
                outs[0][2, :, cut] = jnp.where(swap, first, last)
                if joins:
                    outs[1][part, :, cut] = zero.astype(BF16)
                else:
                    outs[1][:, cut] = zero.astype(BF16)
            for p in range(joins):
                outs[1][p] = refs[n + 2 + p][...]

        got = call(body, [pinned(3, quarter, cols, dtype=F32), one if joins else flat],
                   [VMEM] * (n + 2 + joins) + [ANY],
                   [*taken, sols[part], v["weights"], *near_give0[:joins], v["token"]],
                   flops=8 * quarter * depth * cols)
        v["token"] = got[0]
        near_own.append(got[0])
        if joins:
            v["got0"] = pair_swap(got[1], "col")
        else:
            near_give0.append(got[1])

    for part in range(half):
        near_gives(part)
        near_rest(part)

    def products(far, ks, epilogue, outs, extra, deep=slice(None)):
        n_extra = len(extra)

        def body(*refs):
            far_ref, refs = refs[0], refs[1:]
            sol_refs, weights = refs[:half], refs[half]
            more = refs[half + 1:half + 1 + n_extra]
            out = refs[len(refs) - len(outs):]
            is_odd = on_odd()
            left = far_ref[...].reshape(len(ks) * quarter, far_ref.shape[2])
            for part, sol_ref in enumerate(sol_refs):
                for cut in cuts:
                    total = jnp.dot(left, sol_ref[deep, cut], preferred_element_type=F32)
                    for i, k in enumerate(ks):
                        term = total[i * quarter:(i + 1) * quarter]
                        term = term * weights[pl.ds(tile_of(k, hops), 1), :total.shape[1]]
                        epilogue(out, more, is_odd, i, part, cut, term)

        args = [far, *sols, v["weights"], *extra, v["token"]]
        specs = [VMEM] * (half + 2 + n_extra) + [ANY]
        got = call(body, outs, specs, args, flops=2 * len(ks) * quarter * depth * cols * half)
        v["token"] = got[0]
        return got

    def plain(out, more, is_odd, i, part, cut, total):
        out[0][part, :, cut] = total

    def rounded(out, more, is_odd, i, part, cut, total):
        out[i][part, :, cut] = total.astype(BF16)


    def near2(*refs):
        for p in range(half):
            own, got = refs[p], refs[half + p]
            refs[-1][p] = (own[0] + jnp.where(on_odd(), got[1].astype(F32), got[0].astype(F32))).astype(BF16)

    d2n, = chained(near2, [one], [*near_own, *near_got])
    d2n_in = shift(d2n, "col", 2)

    got_far = [pair_swap(g, "col") for g in products(y24, (2, 4), rounded, [one, one], [])]

    def near3(*refs):
        for p in range(half):
            own, got = refs[p], refs[half + p]
            refs[-1][p] = (own[1] + jnp.where(on_odd(), 0.0, got[1].astype(F32))).astype(BF16)

    d3n, = chained(near3, [one], [*near_own, *near_got])
    d3n_in = shift(d3n, "col", hops)

    def near1(*refs):
        got0, arrived, d1 = refs[2 * half:]
        for p in range(half):
            own, got = refs[p], refs[half + p]
            r = jnp.where(on_odd(), got[0].astype(F32), got0[p].astype(F32))
            d1[p] = (own[2] + r + arrived[p].astype(F32)).astype(BF16)

    d1n, = chained(near1, [one], [*near_own, *near_got, v["got0"], d2n_in])
    d1n_in = shift(d1n, "col", 2)

    def near3_in(d3, got0, out):
        for p in range(half):
            out[p] = d3[p].astype(F32) + jnp.where(on_odd(), got0[p].astype(F32), 0.0)

    near_sum, = chained(near3_in, [wide_one], [d3n_in, v["got0"]])

    def far03(out, more, is_odd, i, part, cut, total):
        r2, r4 = [m[part, :, cut].astype(F32) for m in more]
        if i == 1:
            total = total + jnp.where(is_odd, r4, r2)
        out[i][part, :, cut] = total.astype(BF16)

    last_give, d2f = products(y03, (0, 3), far03, [one, one], got_far)
    got_last, d2f_in = pair_swap(last_give, "col"), shift(d2f, "col", 2)

    def near1_in(d1, sums, out):
        for p in range(half):
            out[p] = d1[p].astype(F32) + sums[p]

    near_all, = chained(near1_in, [wide_one], [d1n_in, near_sum])

    def by_columns(total, *outs):
        for p in range(half):
            outs[p][...] = total[p]

    sums_n = to_columns(chained(by_columns, [pinned(quarter, cols, dtype=F32)] * half, [near_all]), 0)

    raw, = products(y_first, ("first",), plain, [wide_one], [])

    def send(parts, last):
        n = lax.axis_size("col")
        swaps = [n % 4 == 0 and c // 2 % 2 == 1 for c in range(n)]
        far_off = [c + (2 if last != swap else hops) for c, swap in enumerate(swaps)]
        out = []
        for j, part in enumerate(parts):
            route = [(c * size + r, far_off[c] % n * size + inner(r, j, half)) for c in range(n) for r in range(size)]
            out.append(lax.ppermute(part, ("col", "rhs"), route))
        return out

    def far2_in(d2, r2, out):
        for p in range(half):
            out[p] = d2[p].astype(F32) + jnp.where(on_odd(), r2[p].astype(F32), 0.0)

    chain, = chained(far2_in, [wide_one], [d2f_in, got_far[0]])

    def far_first(raw, r4, r0, chain, *refs):
        outs, pre = refs[:half], refs[half]
        is_odd, swap = on_odd(), on_swap()
        for p in range(half):
            one = chain[p] + jnp.where(is_odd, 0.0, r0[p].astype(F32))
            three = jnp.where(is_odd, 0.0, r4[p].astype(F32))
            outs[p][...] = (raw[p] + jnp.where(swap, one, three)).astype(BF16)
            pre[p] = jnp.where(swap, three, one)

    *firsts, pre = chained(far_first, [flat] * half + [wide_one], [raw, got_far[1], got_last, chain])
    first_in = send(firsts, False)

    def far_stay(r0, *outs):
        for p in range(half):
            outs[p][...] = jnp.where(on_odd(), r0[p].astype(F32), 0.0).astype(BF16)

    sums_f = to_columns(chained(far_stay, [flat] * half, [got_last]), 0)

    part1, = products(y_last, ("last",), plain, [wide_one], [], slice(0, middle))

    def added(out, more, is_odd, i, part, cut, total):
        for m in more:
            total = total + m[part, :, cut]
        out[part][:, cut] = total.astype(BF16)

    lasts = products(y_last_rest, ("last",), added, [flat] * half, [part1, pre], slice(middle, depth))
    last_in = send(lasts, True)

    places = [(0, j) for j in range(half)] + [(1, j) for j in range(1, half)] + [(1, 0)]

    def arrange(rhs, diag, _, rhs_out, diag_out):
        me = lax.axis_index("rhs")
        upper, mine = lax.div(me, half), lax.rem(me, half)
        column = lax.broadcasted_iota(jnp.int32, (rows, rows), 1)
        source = column
        for slot, (s, j) in enumerate(places):
            at = slot * quarter
            block = lax.rem(upper + s, 2) * half + lax.rem(mine + half - j, half)
            start = pl.multiple_of(block * quarter, quarter)
            rhs_out[at:at + quarter] = rhs[pl.ds(start, quarter)]
            source = jnp.where((column >= at) & (column < at + quarter), column - at + start, source)
        pick = (lax.broadcasted_iota(jnp.int32, (rows, rows), 0) == source).astype(BF16)
        diag_out[...] = jnp.dot(diag[0], pick, preferred_element_type=F32).astype(BF16)

    rhs_local, diag_local = call(arrange, [pinned(rows, cols), pinned(rows, rows)], [VMEM, VMEM, ANY],
                                 [rhs_block, diag_inverse, near_own[-1]], flops=2 * rows * rows * rows)

    most_rows = rows - quarter

    def gather(*refs):
        near, stay, far, out = refs[:half], refs[half:2 * half], refs[2 * half:3 * half], refs[-1]
        for j in range(half):
            out[j * quarter:(j + 1) * quarter] = near[j][...]
        for j in range(half):
            at = (half + (j - 1) % half) * quarter
            out[at:at + quarter] = stay[j][...].astype(F32) + far[j][...].astype(F32)

    known, = chained(gather, [pinned(rows, cols, dtype=F32)], [*sums_n, *sums_f, *first_in])

    def most(rhs, diag, known, *refs):
        last, out = refs[:half - 1], refs[-1]
        total = jnp.concatenate([known[:rows // 2]] + [known[(half + j) * quarter:(half + j + 1) * quarter]
                                                      + l[...].astype(F32) for j, l in enumerate(last)])
        remaining = (rhs[:most_rows].astype(F32) - total).astype(BF16)
        out[...] = jnp.dot(diag[:, :most_rows], remaining, preferred_element_type=F32)

    partial, = chained(most, [pinned(rows, cols, dtype=F32)], [rhs_local, diag_local, known, *last_in[1:]],
                       flops=2 * rows * most_rows * cols)

    def final(rhs, diag, known, last, part, out, block, sems):
        total = known[most_rows:] + last[...].astype(F32)
        remaining = (rhs[most_rows:].astype(F32) - total).astype(BF16)
        copies = []
        for i in range(size):
            cut = slice(i * quarter, (i + 1) * quarter)
            term = jnp.dot(diag[cut, most_rows:], remaining, preferred_element_type=F32)
            block[cut] = (part[cut] + term).astype(BF16)
            copies.append(pltpu.make_async_copy(block.at[cut], out.at[cut], sems.at[i]))
            copies[-1].start()
        for c in copies:
            c.wait()

    return call(final, [jax.ShapeDtypeStruct((rows, cols), BF16)], [VMEM] * 5,
                [rhs_local, diag_local, known, last_in[0], partial], flops=2 * rows * quarter * cols,
                out_specs=[ANY], scratch_shapes=[pltpu.VMEM((rows, cols), BF16), pltpu.SemaphoreType.DMA((size,))])[0]


def solution(mesh):
    in_specs = (
        P("col", "rhs"),
        P("col", "rhs"),
        P("col", None, "rhs", None),
        P("col", None),
        P("col", None, None),
    )
    out_specs = P("col", "rhs")
    return jax.shard_map(
        per_device, mesh=mesh, in_specs=in_specs, out_specs=out_specs, check_vma=False
    )
```

```python
import functools

import jax
import jax.numpy as jnp
from jax import lax
from jax.experimental import pallas as pl
from jax.experimental.pallas import tpu as pltpu
from jax.sharding import PartitionSpec as P

F32, BF16 = jnp.float32, jnp.bfloat16
VMEM = pl.BlockSpec(memory_space=pltpu.VMEM)
SMEM = pl.BlockSpec(memory_space=pltpu.SMEM)
ANY = pl.BlockSpec(memory_space=pl.ANY)
HBM = pl.BlockSpec(memory_space=pltpu.HBM)


WIDE = 256
PIECES = 4


def shift(block, axis, distance):
    size = lax.axis_size(axis)
    return lax.ppermute(block, axis, [(i, (i + distance) % size) for i in range(size)])


def pair_swap(block, axis):
    size = lax.axis_size(axis)
    return lax.ppermute(block, axis, [(i, i ^ 1) for i in range(size)])


def across(block, axis):
    return shift(block, axis, lax.axis_size(axis) // 2)


def inner(i, j, half):
    return i // half * half + (i % half + j) % half


def half_gather(block, axis):
    size = lax.axis_size(axis)
    half = size // 2
    parts = [block]
    for j in range(1, half):
        parts.append(lax.ppermute(block, axis, [(inner(i, j, half), i) for i in range(size)]))
    return parts


def to_columns(blocks, distance):
    n, size = lax.axis_size("col"), lax.axis_size("rhs")
    out = []
    for j, block in enumerate(blocks):
        route = [(c * size + r, (c + distance) % n * size + inner(r, j, size // 2))
                 for c in range(n) for r in range(size)]
        out.append(lax.ppermute(block, ("col", "rhs"), route) if distance or j else block)
    return out


def pinned(*shape, dtype=BF16):
    return pltpu.VMEM(shape, dtype)


def call(body, outs, specs, args, flops=0, space=12, out_specs=None, **more):
    moved = sum(a.size * a.dtype.itemsize for a in args)
    return pl.pallas_call(
        body,
        out_shape=outs,
        in_specs=specs,
        out_specs=out_specs or [VMEM] * len(outs),
        compiler_params=pltpu.CompilerParams(vmem_limit_bytes=space << 20),
        cost_estimate=pl.CostEstimate(flops=flops, bytes_accessed=moved, transcendentals=0),
        **more,
    )(*args)


def take(tiles, groups, *earlier, weights=None):
    n, rows, depth = len(groups), tiles.shape[1], tiles.shape[2]
    extra = [] if weights is None else [SMEM]

    def body(*refs):
        src, dsts, sems = refs[0], refs[-1 - n - len(extra):-1], refs[-1]
        copies = []
        for group, dst in zip(groups, dsts):
            for i, (k, begin, end) in enumerate(group):
                k = tile_of(k, tiles.shape[0])
                columns = pl.ds(begin, end - begin)
                for first in range(0, rows, rows // PIECES):
                    cut = pl.ds(first, rows // PIECES)
                    copies.append(pltpu.make_async_copy(src.at[k, cut, columns], dst.at[i, cut], sems.at[len(copies)]))
        for c in copies:
            c.start()
        if extra:
            for k in range(weights.shape[1]):
                dsts[-1][k:k + 1, :] = jnp.full((1, WIDE), refs[1][0, k].astype(F32))
        for c in copies:
            c.wait()

    outs = [pinned(len(g), rows, g[0][2] - g[0][1]) for g in groups]
    if extra:
        outs.append(pinned(weights.shape[1], WIDE, dtype=F32))
    return call(body, outs, [HBM] + extra + [ANY] * len(earlier),
                [in_hbm(tiles)] + ([] if weights is None else [in_hbm(weights)]) + [*earlier], space=2,
                scratch_shapes=[pltpu.SemaphoreType.DMA((PIECES * sum(map(len, groups)),))])


def in_hbm(array):
    return pltpu.with_memory_space_constraint(array, pltpu.HBM)


def on_odd():
    return lax.rem(lax.axis_index("col"), 2) == 1


def on_swap():
    if lax.axis_size("col") % 4:
        return jnp.bool_(False)
    return lax.rem(lax.div(lax.axis_index("col"), 2), 2) == 1


def tile_of(k, hops):
    low, high = (1, hops - 1) if k == "first" else (hops - 1, 1)
    return jnp.where(on_swap(), low, high) if isinstance(k, str) else k


def column_cuts(cols):
    wide = min(WIDE, cols)
    return [slice(at, at + wide) for at in range(0, cols, wide)]


def per_device(rhs_block, solution, factor, tile_list, diag_inverse):
    hops, quarter, depth = factor.shape[1:]
    rows, cols = rhs_block.shape
    size = lax.axis_size("rhs")
    half = size // 2
    tiles = factor[0]
    gives, owns = (2, 4, 0), (3, 5, 1)
    cuts = column_cuts(cols)
    strip = (half, quarter, cols)
    one, wide_one = pinned(*strip), pinned(*strip, dtype=F32)
    flat = pinned(quarter, cols)
    v = {}

    s24, = take(tiles, [[(2, 0, depth), (4, 0, depth)]])
    y24 = across(s24, "rhs")
    others = half_gather(solution, "rhs")[1:]
    middle = depth // 2
    sols = [solution, *others]
    v["token"] = s24

    def chained(body, outs, ins, flops=0):
        n = len(ins)

        def run(*refs):
            body(*refs[:n], *refs[n + 1:])

        got = call(run, outs, [VMEM] * n + [ANY], [*ins, v["token"]], flops=flops)
        v["token"] = got[0]
        return got

    order = (0, 3, "first", "last")
    groups = [[(0, 0, depth), (3, 0, depth)], [("first", 0, depth)], [("last", 0, middle)], [("last", middle, depth)]]
    *taken, v["weights"] = take(tiles, groups, s24, weights=tile_list)
    y03, y_first, y_last, y_last_rest = [across(s, "rhs") for s in taken]
    v["token"] = taken[0]

    near_got, near_own, near_give0 = [], [], []

    def near_gives(part):
        def body(*refs):
            left_ref, sol, weights, _, give = refs
            left = left_ref[...].reshape(2 * quarter, depth)
            for cut in cuts:
                total = jnp.dot(left, sol[:, cut], preferred_element_type=F32)
                for i in range(2):
                    term = total[i * quarter:(i + 1) * quarter] * weights[gives[i]:gives[i] + 1, :total.shape[1]]
                    give[i, :, cut] = term.astype(BF16)

        got = call(body, [pinned(2, quarter, cols)], [VMEM] * 3 + [ANY],
                   [s24, sols[part], v["weights"], v["token"]], flops=4 * quarter * depth * cols)
        v["token"] = got[0]
        near_got.append(pair_swap(got[0], "col"))

    def near_rest(part):
        n = len(taken)
        joins = half - 1 if part == half - 1 else 0

        def body(*refs):
            lefts, (sol, weights), outs = refs[:n], refs[n:n + 2], refs[n + 3 + joins:]
            whole = [r[i] for r in lefts[:2] for i in range(r.shape[0])]
            left = jnp.concatenate(whole + [jnp.concatenate([r[0] for r in lefts[2:]], axis=1)])
            swap = on_swap()
            for cut in cuts:
                total = jnp.dot(left, sol[:, cut], preferred_element_type=F32)
                zero, three, first, last = [
                    total[at * quarter:(at + 1) * quarter] * weights[pl.ds(tile_of(k, hops), 1), :total.shape[1]]
                    for at, k in enumerate(order)]
                outs[0][0, :, cut] = three
                outs[0][1, :, cut] = jnp.where(swap, last, first)
                outs[0][2, :, cut] = jnp.where(swap, first, last)
                if joins:
                    outs[1][part, :, cut] = zero.astype(BF16)
                else:
                    outs[1][:, cut] = zero.astype(BF16)
            for p in range(joins):
                outs[1][p] = refs[n + 2 + p][...]

        got = call(body, [pinned(3, quarter, cols, dtype=F32), one if joins else flat],
                   [VMEM] * (n + 2 + joins) + [ANY],
                   [*taken, sols[part], v["weights"], *near_give0[:joins], v["token"]],
                   flops=8 * quarter * depth * cols)
        v["token"] = got[0]
        near_own.append(got[0])
        if joins:
            v["got0"] = pair_swap(got[1], "col")
        else:
            near_give0.append(got[1])

    for part in range(half):
        near_gives(part)
        near_rest(part)

    def products(far, ks, epilogue, outs, extra, deep=slice(None)):
        n_extra = len(extra)

        def body(*refs):
            far_ref, refs = refs[0], refs[1:]
            sol_refs, weights = refs[:half], refs[half]
            more = refs[half + 1:half + 1 + n_extra]
            out = refs[len(refs) - len(outs):]
            is_odd = on_odd()
            left = far_ref[...].reshape(len(ks) * quarter, far_ref.shape[2])
            for part, sol_ref in enumerate(sol_refs):
                for cut in cuts:
                    total = jnp.dot(left, sol_ref[deep, cut], preferred_element_type=F32)
                    for i, k in enumerate(ks):
                        term = total[i * quarter:(i + 1) * quarter]
                        term = term * weights[pl.ds(tile_of(k, hops), 1), :total.shape[1]]
                        epilogue(out, more, is_odd, i, part, cut, term)

        args = [far, *sols, v["weights"], *extra, v["token"]]
        specs = [VMEM] * (half + 2 + n_extra) + [ANY]
        got = call(body, outs, specs, args, flops=2 * len(ks) * quarter * depth * cols * half)
        v["token"] = got[0]
        return got

    def plain(out, more, is_odd, i, part, cut, total):
        out[0][part, :, cut] = total

    def rounded(out, more, is_odd, i, part, cut, total):
        out[i][part, :, cut] = total.astype(BF16)


    def near2(*refs):
        for p in range(half):
            own, got = refs[p], refs[half + p]
            refs[-1][p] = (own[0] + jnp.where(on_odd(), got[1].astype(F32), got[0].astype(F32))).astype(BF16)

    d2n, = chained(near2, [one], [*near_own, *near_got])
    d2n_in = shift(d2n, "col", 2)

    got_far = [pair_swap(g, "col") for g in products(y24, (2, 4), rounded, [one, one], [])]

    def near3(*refs):
        for p in range(half):
            own, got = refs[p], refs[half + p]
            refs[-1][p] = (own[1] + jnp.where(on_odd(), 0.0, got[1].astype(F32))).astype(BF16)

    d3n, = chained(near3, [one], [*near_own, *near_got])
    d3n_in = shift(d3n, "col", hops)

    def near1(*refs):
        got0, arrived, d1 = refs[2 * half:]
        for p in range(half):
            own, got = refs[p], refs[half + p]
            r = jnp.where(on_odd(), got[0].astype(F32), got0[p].astype(F32))
            d1[p] = (own[2] + r + arrived[p].astype(F32)).astype(BF16)

    d1n, = chained(near1, [one], [*near_own, *near_got, v["got0"], d2n_in])
    d1n_in = shift(d1n, "col", 2)

    def near3_in(d3, got0, out):
        for p in range(half):
            out[p] = d3[p].astype(F32) + jnp.where(on_odd(), got0[p].astype(F32), 0.0)

    near_sum, = chained(near3_in, [wide_one], [d3n_in, v["got0"]])

    def far03(out, more, is_odd, i, part, cut, total):
        r2, r4 = [m[part, :, cut].astype(F32) for m in more]
        if i == 1:
            total = total + jnp.where(is_odd, r4, r2)
        out[i][part, :, cut] = total.astype(BF16)

    last_give, d2f = products(y03, (0, 3), far03, [one, one], got_far)
    got_last, d2f_in = pair_swap(last_give, "col"), shift(d2f, "col", 2)

    def near1_in(d1, sums, out):
        for p in range(half):
            out[p] = d1[p].astype(F32) + sums[p]

    near_all, = chained(near1_in, [wide_one], [d1n_in, near_sum])

    def by_columns(total, *outs):
        for p in range(half):
            outs[p][...] = total[p]

    sums_n = to_columns(chained(by_columns, [pinned(quarter, cols, dtype=F32)] * half, [near_all]), 0)

    raw, = products(y_first, ("first",), plain, [wide_one], [])

    def send(parts, last):
        n = lax.axis_size("col")
        swaps = [n % 4 == 0 and c // 2 % 2 == 1 for c in range(n)]
        far_off = [c + (2 if last != swap else hops) for c, swap in enumerate(swaps)]
        out = []
        for j, part in enumerate(parts):
            route = [(c * size + r, far_off[c] % n * size + inner(r, j, half)) for c in range(n) for r in range(size)]
            out.append(lax.ppermute(part, ("col", "rhs"), route))
        return out

    def far2_in(d2, r2, out):
        for p in range(half):
            out[p] = d2[p].astype(F32) + jnp.where(on_odd(), r2[p].astype(F32), 0.0)

    chain, = chained(far2_in, [wide_one], [d2f_in, got_far[0]])

    def far_first(raw, r4, r0, chain, *refs):
        outs, pre = refs[:half], refs[half]
        is_odd, swap = on_odd(), on_swap()
        for p in range(half):
            one = chain[p] + jnp.where(is_odd, 0.0, r0[p].astype(F32))
            three = jnp.where(is_odd, 0.0, r4[p].astype(F32))
            outs[p][...] = (raw[p] + jnp.where(swap, one, three)).astype(BF16)
            pre[p] = jnp.where(swap, three, one)

    *firsts, pre = chained(far_first, [flat] * half + [wide_one], [raw, got_far[1], got_last, chain])
    first_in = send(firsts, False)

    def far_stay(r0, *outs):
        for p in range(half):
            outs[p][...] = jnp.where(on_odd(), r0[p].astype(F32), 0.0).astype(BF16)

    sums_f = to_columns(chained(far_stay, [flat] * half, [got_last]), 0)

    part1, = products(y_last, ("last",), plain, [wide_one], [], slice(0, middle))

    def added(out, more, is_odd, i, part, cut, total):
        for m in more:
            total = total + m[part, :, cut]
        out[part][:, cut] = total.astype(BF16)

    lasts = products(y_last_rest, ("last",), added, [flat] * half, [part1, pre], slice(middle, depth))
    last_in = send(lasts, True)

    places = [(0, j) for j in range(half)] + [(1, j) for j in range(1, half)] + [(1, 0)]

    def arrange(rhs, diag, _, rhs_out, diag_out):
        me = lax.axis_index("rhs")
        upper, mine = lax.div(me, half), lax.rem(me, half)
        column = lax.broadcasted_iota(jnp.int32, (rows, rows), 1)
        source = column
        for slot, (s, j) in enumerate(places):
            at = slot * quarter
            block = lax.rem(upper + s, 2) * half + lax.rem(mine + half - j, half)
            start = pl.multiple_of(block * quarter, quarter)
            rhs_out[at:at + quarter] = rhs[pl.ds(start, quarter)]
            source = jnp.where((column >= at) & (column < at + quarter), column - at + start, source)
        pick = (lax.broadcasted_iota(jnp.int32, (rows, rows), 0) == source).astype(BF16)
        diag_out[...] = jnp.dot(diag[0], pick, preferred_element_type=F32).astype(BF16)

    rhs_local, diag_local = call(arrange, [pinned(rows, cols), pinned(rows, rows)], [VMEM, VMEM, ANY],
                                 [rhs_block, diag_inverse, near_own[-1]], flops=2 * rows * rows * rows)

    most_rows = rows - quarter

    def gather(*refs):
        near, stay, far, out = refs[:half], refs[half:2 * half], refs[2 * half:3 * half], refs[-1]
        for j in range(half):
            out[j * quarter:(j + 1) * quarter] = near[j][...]
        for j in range(half):
            at = (half + (j - 1) % half) * quarter
            out[at:at + quarter] = stay[j][...].astype(F32) + far[j][...].astype(F32)

    known, = chained(gather, [pinned(rows, cols, dtype=F32)], [*sums_n, *sums_f, *first_in])

    def most(rhs, diag, known, *refs):
        last, out = refs[:half - 1], refs[-1]
        total = jnp.concatenate([known[:rows // 2]] + [known[(half + j) * quarter:(half + j + 1) * quarter]
                                                      + l[...].astype(F32) for j, l in enumerate(last)])
        remaining = (rhs[:most_rows].astype(F32) - total).astype(BF16)
        out[...] = jnp.dot(diag[:, :most_rows], remaining, preferred_element_type=F32)

    partial, = chained(most, [pinned(rows, cols, dtype=F32)], [rhs_local, diag_local, known, *last_in[1:]],
                       flops=2 * rows * most_rows * cols)

    def final(rhs, diag, known, last, part, out, block, sems):
        total = known[most_rows:] + last[...].astype(F32)
        remaining = (rhs[most_rows:].astype(F32) - total).astype(BF16)
        copies = []
        for i in range(size):
            cut = slice(i * quarter, (i + 1) * quarter)
            term = jnp.dot(diag[cut, most_rows:], remaining, preferred_element_type=F32)
            block[cut] = (part[cut] + term).astype(BF16)
            copies.append(pltpu.make_async_copy(block.at[cut], out.at[cut], sems.at[i]))
            copies[-1].start()
        for c in copies:
            c.wait()

    return call(final, [jax.ShapeDtypeStruct((rows, cols), BF16)], [VMEM] * 5,
                [rhs_local, diag_local, known, last_in[0], partial], flops=2 * rows * quarter * cols,
                out_specs=[ANY], scratch_shapes=[pltpu.VMEM((rows, cols), BF16), pltpu.SemaphoreType.DMA((size,))])[0]


def solution(mesh):
    in_specs = (
        P("col", "rhs"),
        P("col", "rhs"),
        P("col", None, "rhs", None),
        P("col", None),
        P("col", None, None),
    )
    out_specs = P("col", "rhs")
    return jax.shard_map(
        per_device, mesh=mesh, in_specs=in_specs, out_specs=out_specs, check_vma=False
    )
```
